32 devices in a mesh: grp: 2 (over y), dp: 8 (over z, x), space: 2 (over core).
Axes of the slice: x: 2, y: 2, z: 4, core: 2. Of those that a mesh axis runs over, the one named last changes fastest.
Arguments:
- inputs: bfloat16 [16, 32, 64, 512], P(('grp', 'dp'), 'space'), parts along dimension 0, may hold values from -6 to 6
- cotangent: bfloat16 [16, 32, 64, 512], P(('grp', 'dp'), 'space'), parts along dimension 0, may hold values from -6 to 6
- spectral_weight: float32 [4, 128, 9, 64, 128], P(('grp', 'space'), 'dp'), parts along dimension 0, may hold values from -0.5 to 0.5
- first_moment: float32 [4, 128, 9, 64, 128], P(('grp', 'space'), 'dp'), parts along dimension 0, may hold values from -18 to 18
- second_moment: float32 [4, 128, 9, 64, 128], P(('grp', 'space'), 'dp'), parts along dimension 0, may hold values from 1 to 100
- pointwise_weight: float32 [128, 64], P('grp'), parts along dimension 0, may hold values from -0.75 to 0.75
Outputs:
- grad_input: bfloat16 [16, 32, 64, 512], P(('grp', 'dp'), 'space'), parts along dimension 0
- new_weight: float32 [4, 128, 9, 64, 128], P(('grp', 'space'), 'dp'), parts along dimension 0
- new_first: float32 [4, 128, 9, 64, 128], P(('grp', 'space'), 'dp'), parts along dimension 0
- new_second: float32 [4, 128, 9, 64, 128], P(('grp', 'space'), 'dp'), parts along dimension 0
The draws below stay inside these ranges and needn't reach their ends.
There are 2 independent parts, one for each index of `grp`. The reference program is written for one: setup_inputs(seed, part) draws one part's arguments, and reference() takes and returns one part's arrays. A program takes and returns all parts, laid end to end along the dimension named above; each array names one. Nothing has to cross between parts.
All inputs are finite; a program needn't handle non-finite values.
Results may differ from the reference program's by a relative error of at most 0.001.
Values sent between devices are 32-bit elements; how exact they have to be, the bound alone decides.
No kernel may reach another device: no remote copies, remote signals or barrier semaphores. Data moves between devices by JAX's collectives and lax.ppermute only.
A program may use at most 128 MiB of HBM per device.

```python
import math
import jax
import jax.numpy as jnp
from jax import lax

CH = 64
MX = 16
MY = 16
MZ = 9
GX = 32
GY = 16
GZ = 32
SAMPLES = 8
YGROUPS = 2
PAIRS = 128
YZ = 512


def shard_levels(stream_key, shape, shards, smallest, high):
    def one(axis_at, shards_of):
        draws = jax.random.uniform(jax.random.fold_in(jax.random.fold_in(stream_key, 6), axis_at), (shards_of,), jnp.float32, smallest / len(shards), high / len(shards))
        return jnp.repeat(jnp.exp(draws), shape[axis_at] // shards_of).reshape((-1,) + (1,) * (len(shape) - axis_at - 1))

    loudness = one(*shards[0])
    for cut in shards[1:]:
        loudness = loudness * one(*cut)
    return loudness


def gaussian(stream_key, extent, scale, limit, pieces=(), held_as=jnp.bfloat16):
    array = jax.random.normal(stream_key, extent, jnp.float32) * scale
    if len(pieces) > 0:
        array = shard_levels(stream_key, extent, pieces, -0.22, 0.18) * array
    return jnp.clip(array, min=-limit, max=limit).astype(held_as)


def setup_inputs(seed: int = 0, part: int = 0) -> dict:
    streams_of = jax.random.split(jax.random.key(seed), 7)
    part_keys = jax.random.split(jax.random.fold_in(streams_of[6], part), 7)
    inputs = gaussian(part_keys[0], (SAMPLES, GX, CH, YZ), 1.0, 6.0, ((0, 8), (1, 2)))
    cotangent = gaussian(part_keys[1], (SAMPLES, GX, CH, YZ), 1.0, 6.0, ((0, 8), (1, 2)))
    spectral_weight = gaussian(part_keys[2], (YGROUPS, PAIRS, MZ, CH, 2 * CH), (2 * CH) ** -0.5, 0.5, ((0, 2), (1, 8)), jnp.float32)
    first_moment = gaussian(part_keys[3], (YGROUPS, PAIRS, MZ, CH, 2 * CH), 3.0, 18.0, ((0, 2), (1, 8)), jnp.float32)
    second_moment = jnp.clip(jnp.exp(math.log(100.0) - 4.6051702 * jax.random.uniform(part_keys[4], (YGROUPS, PAIRS, MZ, CH, 2 * CH), jnp.float32) ** shard_levels(part_keys[4], (YGROUPS, PAIRS, MZ, CH, 2 * CH), ((0, 2), (1, 8)), -0.2, 0.2)), 1.0, 100.0)
    pointwise_weight = gaussian(part_keys[5], (CH, CH), CH ** -0.5, 0.75, (), jnp.float32)
    return dict(inputs=inputs, cotangent=cotangent, spectral_weight=spectral_weight, first_moment=first_moment, second_moment=second_moment, pointwise_weight=pointwise_weight)


beta_first = 0.9
beta_second = 0.999
learn_rate = 0.001
adam_epsilon = 1e-08
first_correct = 1.0 - math.exp(1000.0 * math.log(0.9))
second_correct = 1.0 - math.exp(1000.0 * math.log(0.999))

def kept_frequencies(count, length):
    return jnp.concatenate([jnp.arange(count // 2), jnp.arange(length - count // 2, length)]).astype(jnp.int32)

def complex_weight(weight):
    joined = weight[..., :CH] + 1j * weight[..., CH:]
    joined = joined.reshape(YGROUPS, MX, MY // YGROUPS, MZ, CH, CH)
    return jnp.transpose(joined, (1, 0, 2, 3, 4, 5)).reshape(MX, MY, MZ, CH, CH)

def layer(input_field, weight, pointwise_weight):
    x_frequencies = kept_frequencies(MX, GX)
    y_frequencies = kept_frequencies(MY, GY)
    volume = input_field.reshape(GX, CH, GY, GZ)
    spectrum = jnp.fft.rfftn(volume, axes=(0, 2, 3))
    kept = spectrum[x_frequencies][:, :, y_frequencies][:, :, :, :MZ]
    mixture = jnp.einsum('xiyz,xyzio->xoyz', kept, complex_weight(weight), precision=lax.Precision.HIGHEST)
    padded = jnp.zeros((GX, CH, MY, MZ), mixture.dtype).at[x_frequencies].set(mixture)
    padded = jnp.zeros((GX, CH, GY, MZ), mixture.dtype).at[:, :, y_frequencies].set(padded)
    padded = jnp.pad(padded, ((0, 0), (0, 0), (0, 0), (0, GZ // 2 + 1 - MZ)))
    spatial_term = jnp.fft.irfftn(padded, s=(GX, GY, GZ), axes=(0, 2, 3)).reshape(GX, CH, GY * GZ)
    local_term = jnp.einsum('xir,io->xor', input_field, pointwise_weight, precision=lax.Precision.HIGHEST)
    return jax.nn.gelu(spatial_term + local_term)

def reference(inputs, cotangent, spectral_weight, first_moment, second_moment, pointwise_weight):

    def one_sample(total, couple):
        input_field = couple[0].astype(jnp.float32)
        upstream = couple[1].astype(jnp.float32)
        result, backward = jax.vjp(lambda entry, weight: layer(entry, weight, pointwise_weight), input_field, spectral_weight)
        field_gradient, grad_weight = backward(upstream)
        return (total + grad_weight, field_gradient.astype(jnp.bfloat16))
    gradient, grad_input = lax.scan(one_sample, jnp.zeros(spectral_weight.shape, jnp.float32), (inputs, cotangent))
    new_first = beta_first * first_moment + (1.0 - beta_first) * gradient
    new_second = beta_second * second_moment + (1.0 - beta_second) * gradient * gradient
    update = learn_rate * (new_first / first_correct) / (jnp.sqrt(new_second / second_correct) + adam_epsilon)
    new_weight = spectral_weight - update
    return (grad_input, new_weight, new_first, new_second)
```

```python
import math

import jax
import jax.numpy as jnp
import ml_dtypes
import numpy as np
from jax import lax
from jax.experimental import pallas as pl
from jax.experimental.pallas import tpu as pltpu
from jax.sharding import PartitionSpec as P

MX = 16
MY = 16
MZ = 9
GX = 32
GY = 16
GZ = 32
HALF = MX // 2 + 1
CBLOCK = 16

beta_first = 0.9
beta_second = 0.999
learn_rate = 0.001
adam_epsilon = 1e-08
first_correct = 1.0 - math.exp(1000.0 * math.log(0.9))
second_correct = 1.0 - math.exp(1000.0 * math.log(0.999))

f32 = jnp.float32
bf16 = jnp.bfloat16


def split_np(table):
    high = table.astype(np.float32).astype(ml_dtypes.bfloat16)
    low = (table - high.astype(np.float64)).astype(np.float32).astype(ml_dtypes.bfloat16)
    return high, low


def yz_tables(groups, scaled):
    per_group = MY // groups
    y_frequency = np.concatenate([np.arange(MY // 2), np.arange(GY - MY // 2, GY)]).reshape(groups, per_group)
    y_place = np.repeat(np.arange(GY), GZ)
    z_place = np.tile(np.arange(GZ), GY)
    turns = y_frequency[:, :, None, None] * y_place / GY + np.arange(MZ)[None, None, :, None] * z_place / GZ
    angle = 2.0 * np.pi * (turns % 1.0)
    table = np.stack([np.cos(angle), -np.sin(angle)], axis=1)
    if scaled:
        table = table * (np.where(np.arange(MZ) == 0, 1.0, 2.0) / (GX * GY * GZ))[:, None]
    table = table.reshape(groups, 2 * per_group * MZ, GY * GZ)
    return np.concatenate(split_np(table), axis=1)


def x_tables(groups):
    width = GX // groups
    place = np.arange(GX).reshape(groups, 1, width)
    angle = 2.0 * np.pi * (np.arange(HALF)[None, :, None] * place % GX) / GX
    table = np.stack([np.cos(angle), -np.sin(angle)], axis=2).reshape(groups, 2 * HALF, width)
    wide = np.einsum("gkx,cd->gkcxd", table, np.eye(CBLOCK)).reshape(groups, 2 * HALF * CBLOCK, width * CBLOCK)
    high, low = split_np(wide)
    forward = np.concatenate([high, low, high], axis=2)
    flip = lambda t: np.swapaxes(t, 1, 2)
    inverse = np.concatenate([flip(high), flip(low), flip(high)], axis=2)
    return forward, np.ascontiguousarray(inverse)


def dot(a, b):
    return lax.dot_general(a, b, (((1,), (0,)), ((), ())), preferred_element_type=f32)


def dot_nt(a, b):
    return lax.dot_general(a, b, (((1,), (1,)), ((), ())), preferred_element_type=f32)


def dot_tn(a, b):
    return lax.dot_general(a, b, (((0,), (0,)), ((), ())), preferred_element_type=f32)


def split(value):
    high = value.astype(bf16)
    return high, (value - high.astype(f32)).astype(bf16)


def lane_sign(shape, first):
    lane = lax.broadcasted_iota(jnp.int32, shape, len(shape) - 1)
    return jnp.where(lane < shape[-1] // 2, first, -first).astype(f32)


def swap(value):
    return pltpu.roll(value, value.shape[-1] // 2, value.ndim - 1)


def to_spectra(channels, fields, x_table, own, other, own_out, other_out, u_high, u_low):
    cells = x_table.shape[1] // 3
    for block in range(channels // CBLOCK):
        pieces = fields(block)
        stacked = pieces[0] if len(pieces) == 1 else jnp.concatenate(pieces, axis=0)
        result = dot(x_table[:, : cells * len(pieces)], stacked)
        high, low = split(result)
        rows = pl.ds(block * CBLOCK, CBLOCK)
        shape = (2 * HALF, CBLOCK, high.shape[-1])
        u_high[:, rows, :] = high.reshape(shape)
        u_low[:, rows, :] = low.reshape(shape)
    table = jnp.concatenate([own[...], other[...]], axis=0)
    part = own.shape[0] // 2
    count = part // 2
    brief = jnp.concatenate([own[:part, :], other[:part, :]], axis=0)
    width = 2 * channels
    sign = lane_sign((count, width), -1.0)
    for first in range(0, HALF, 2):
        several = min(2, HALF - first)
        at = pl.ds(2 * first, 2 * several)
        high = u_high[at].reshape(several * width, u_high.shape[-1])
        low = u_low[at].reshape(several * width, u_low.shape[-1])
        wide = dot_nt(table, high)
        small = dot_nt(brief, low)
        for which, out in enumerate((own_out, other_out)):
            base = 2 * part * which
            total = (wide[base : base + part] + wide[base + part : base + 2 * part]) + small[
                part * which : part * (which + 1)
            ]
            for step in range(several):
                kx = first + step
                real = total[:count, step * width : (step + 1) * width]
                imag = swap(total[count:, step * width : (step + 1) * width])
                if kx < MX // 2:
                    out[kx] = real + imag * sign
                if kx > 0:
                    out[MX - kx] = imag - real * sign


def from_spectra(channels, own_in, other_in, x_table, own, other, u_high, u_low, t_high, t_low):
    part = own.shape[0] // 2
    count = part // 2
    width = 2 * channels
    sign = lane_sign((count, width), -1.0)
    for kx in range(HALF):
        pieces = []
        for source in (own_in, other_in):
            if kx == 0:
                ahead = source[0]
                real, imag = ahead, ahead * sign
            elif kx == MX // 2:
                behind = source[MX - kx]
                real, imag = -behind * sign, behind
            else:
                ahead, behind = source[kx], source[MX - kx]
                real, imag = ahead - behind * sign, ahead * sign + behind
            pieces += [real, swap(imag)]
        turned = jnp.concatenate(pieces, axis=0).T
        high, low = split(turned)
        t_high[pl.ds(kx * width, width), :] = high
        t_low[pl.ds(kx * width, width), :] = low
    table_high = jnp.concatenate([own[:part, :], other[:part, :]], axis=0)
    table_low = jnp.concatenate([own[part:, :], other[part:, :]], axis=0)
    several = 3 if HALF % 3 == 0 else 1
    for first in range(0, HALF, several):
        at = pl.ds(first * width, several * width)
        high, low = t_high[at, :], t_low[at, :]
        value = dot(high, table_high) + dot(low, table_high) + dot(high, table_low)
        value_high, value_low = split(value)
        shape = (2 * several, channels, value.shape[-1])
        u_high[pl.ds(2 * first, 2 * several)] = value_high.reshape(shape)
        u_low[pl.ds(2 * first, 2 * several)] = value_low.reshape(shape)

    def block(index):
        rows = pl.ds(index * CBLOCK, CBLOCK)
        shape = (2 * HALF * CBLOCK, u_high.shape[-1])
        high = u_high[:, rows, :].reshape(shape)
        low = u_low[:, rows, :].reshape(shape)
        return dot(x_table[...], jnp.concatenate([high, high, low], axis=0))

    return block


def first_kernel(place, field, x_table, own, other, own_out, other_out, u_high, u_low):
    width, channels, cells = field.shape

    def fields(block):
        piece = field[:, pl.ds(block * CBLOCK, CBLOCK), :].reshape(width * CBLOCK, cells)
        return [piece, piece]

    to_spectra(channels, fields, x_table, own, other, own_out, other_out, u_high, u_low)


def middle_kernel(
    place, own_in, other_in, field, cotangent, pointwise, x_inverse, x_forward, own, other,
    own_out, other_out, slope_high, slope_low, u_high, u_low, t_high, t_low, pre,
):
    width, channels, cells = field.shape
    block = from_spectra(channels, own_in, other_in, x_inverse, own, other, u_high, u_low, t_high, t_low)
    for index in range(channels // CBLOCK):
        pre[:, pl.ds(index * CBLOCK, CBLOCK), :] = block(index).reshape(width, CBLOCK, cells)
    root = math.sqrt(2.0 / math.pi)
    mixer = jnp.concatenate(split(pointwise[...].T), axis=0)

    @pl.loop(0, width)
    def _(x):
        local = dot(mixer, field[x])
        value = pre[x] + (local[:channels] + local[channels:])
        square = value * value
        tanh = jnp.tanh(root * value * (1.0 + 0.044715 * square))
        slope = 0.5 * (1.0 + tanh) + (0.5 * root) * value * (1.0 - tanh * tanh) * (1.0 + 3.0 * 0.044715 * square)
        slope = slope * cotangent[x].astype(f32)
        high, low = split(slope)
        slope_high[x] = high
        slope_low[x] = low

    def fields(index):
        rows = pl.ds(index * CBLOCK, CBLOCK)
        shape = (width * CBLOCK, cells)
        high = slope_high[:, rows, :].reshape(shape)
        return [high, high, slope_low[:, rows, :].reshape(shape)]

    to_spectra(channels, fields, x_forward, own, other, own_out, other_out, u_high, u_low)


def last_kernel(place, own_in, other_in, local, x_inverse, own, other, out, u_high, u_low, t_high, t_low):
    width, channels, cells = out.shape
    block = from_spectra(channels, own_in, other_in, x_inverse, own, other, u_high, u_low, t_high, t_low)
    for index in range(channels // CBLOCK):
        rows = pl.ds(index * CBLOCK, CBLOCK)
        value = block(index).reshape(width, CBLOCK, cells) + local[:, rows, :]
        out[:, rows, :] = value.astype(bf16)


def local_kernel(high_in, low_in, pointwise, out):
    channels = pointwise.shape[0]
    high, low = split(pointwise[...])
    wide = dot(jnp.concatenate([high, low], axis=0), high_in[0])
    out[0] = (wide[:channels] + wide[channels:]) + dot(high, low_in[0])


def pairs_of(count):
    return [list(range(first, min(first + 2, count))) for first in range(0, count, 2)]


def spread_rows(rows, lower):
    if len(rows) == 1:
        half = rows[0].shape[-1] // 2
        return jnp.concatenate([rows[0][:, :half], rows[0][:, half:]], axis=0)
    zero = jnp.zeros_like(rows[0])
    one, two = rows
    return jnp.concatenate(
        [
            jnp.where(lower, one, zero),
            jnp.where(lower, swap(one), zero),
            jnp.where(lower, zero, swap(two)),
            jnp.where(lower, zero, two),
        ],
        axis=0,
    )


def lower_half(shape):
    return lax.broadcasted_iota(jnp.int32, shape, 1) < shape[1] // 2


def mix_kernel(spectra, weight, out):
    samples, modes, width = spectra.shape
    lower = lower_half((samples, width))
    sign = lane_sign((samples, width), -1.0)
    for group in pairs_of(modes):
        rows = spread_rows([spectra[:, mode, :] for mode in group], lower)
        high, low = split(rows)
        block = weight[group[0] : group[0] + len(group)].reshape(-1, width)
        block_high, block_low = split(block)
        wide = dot(jnp.concatenate([high, low], axis=0), block_high)
        total = wide[: rows.shape[0]] + wide[rows.shape[0] :] + dot(high, block_low)
        for step, mode in enumerate(group):
            base = 2 * samples * step
            real, imag = total[base : base + samples], total[base + samples : base + 2 * samples]
            out[:, mode, :] = real + swap(imag) * sign


def adjoint_kernel(spectra, weight, out):
    samples, modes, width = spectra.shape
    lower = lower_half((samples, width))
    sign = lane_sign((samples, width), 1.0)
    for group in pairs_of(modes):
        rows = []
        for mode in group:
            row = spectra[:, mode, :]
            rows += [row, swap(row) * sign]
        rows = jnp.concatenate(rows, axis=0)
        high, low = split(rows)
        block = weight[group[0] : group[0] + len(group)].reshape(-1, width)
        block_high, block_low = split(block)
        wide = dot_nt(jnp.concatenate([high, low], axis=0), block_high)
        total = wide[: rows.shape[0]] + wide[rows.shape[0] :] + dot_nt(high, block_low)
        if len(group) == 1:
            total = jnp.concatenate([total, total], axis=1)
        for step, mode in enumerate(group):
            base = 2 * samples * step
            real, imag = total[base : base + samples], total[base + samples : base + 2 * samples]
            if len(group) == 1:
                out[:, mode, :] = jnp.where(lower, real, imag)
            elif step == 0:
                out[:, mode, :] = jnp.where(lower, real, swap(imag))
            else:
                out[:, mode, :] = jnp.where(lower, swap(real), imag)


def adam_kernel(spectra, slopes, weight, first, second, weight_out, first_out, second_out):
    samples, modes, width = spectra.shape
    lower = lower_half((samples, width))
    sign = lane_sign((samples, width), 1.0)
    for group in pairs_of(modes):
        left = spread_rows([spectra[:, mode, :] for mode in group], lower)
        right = []
        for mode in group:
            row = slopes[:, mode, :]
            right += [row, swap(row) * sign]
        right = jnp.concatenate(right, axis=0)
        left_high, left_low = split(left)
        right_high, right_low = split(right)
        gradient = dot_tn(
            jnp.concatenate([left_high, left_low, left_high], axis=0),
            jnp.concatenate([right_high, right_high, right_low], axis=0),
        )
        at = pl.ds(group[0], len(group))
        shape = (len(group),) + weight.shape[1:]
        gradient = gradient.reshape(shape)
        new_first = beta_first * first[at] + (1.0 - beta_first) * gradient
        new_second = beta_second * second[at] + (1.0 - beta_second) * gradient * gradient
        bottom = jnp.sqrt(new_second * (1.0 / second_correct)) + adam_epsilon
        first_out[at] = new_first
        second_out[at] = new_second
        weight_out[at] = weight[at] - (learn_rate / first_correct) * new_first / bottom


def body(inputs, cotangent, spectral_weight, first_moment, second_moment, pointwise_weight):
    groups = lax.axis_size("space")
    owners = lax.axis_size("dp")
    assert groups == 2 and inputs.shape[0] == 1
    per_group = MY // groups
    _, width, channels, cells = inputs.shape
    lanes = 2 * channels
    count = per_group * MZ
    pairs = spectral_weight.shape[1]
    modes = pairs * MZ
    place = lax.axis_index("space").astype(jnp.int32).reshape(1)

    plain_table = jnp.asarray(yz_tables(groups, False))
    scaled_table = jnp.asarray(yz_tables(groups, True))
    x_forward, x_inverse = map(jnp.asarray, x_tables(groups))

    def mine(array):
        return pl.BlockSpec((None,) + array.shape[1:], lambda i, s: (s[0], 0, 0))

    def others(array):
        return pl.BlockSpec((None,) + array.shape[1:], lambda i, s: (1 - s[0], 0, 0))

    def entire(shape):
        return pl.BlockSpec(shape, lambda i, s: (0,) * len(shape))

    sample = pl.BlockSpec((None, width, channels, cells), lambda i, s: (0, 0, 0, 0))
    spectrum_shape = (MX, count, lanes)
    spectrum = jax.ShapeDtypeStruct(spectrum_shape, f32)
    field_shape = (width, channels, cells)
    u_scratch = [pltpu.VMEM((2 * HALF, channels, cells), bf16)] * 2
    t_scratch = [pltpu.VMEM((HALF * lanes, 2 * groups * count), bf16)] * 2
    params = pltpu.CompilerParams(vmem_limit_bytes=36 * 1024 * 1024)

    def other_core(value):
        return lax.ppermute(value, "space", [(0, 1), (1, 0)])

    def exchange(value):
        return lax.all_to_all(value, "dp", split_axis=0, concat_axis=0, tiled=True)

    own, sent = pl.pallas_call(
        first_kernel,
        out_shape=[spectrum, spectrum],
        grid_spec=pltpu.PrefetchScalarGridSpec(
            num_scalar_prefetch=1,
            grid=(1,),
            in_specs=[sample, mine(x_forward), mine(plain_table), others(plain_table)],
            out_specs=[entire(spectrum_shape)] * 2,
            scratch_shapes=u_scratch,
        ),
        compiler_params=params,
        name="first",
    )(place, inputs, x_forward, plain_table, plain_table)
    owned = exchange((own + other_core(sent)).reshape(owners, modes, lanes))

    block = 16 if modes % 16 == 0 else modes
    grid = (modes // block,)
    spectra_spec = pl.BlockSpec((owners, block, lanes), lambda i: (0, i, 0))
    weight_shape = (modes, channels, lanes)
    weight_spec = pl.BlockSpec((block, channels, lanes), lambda i: (i, 0, 0))
    weight = spectral_weight.reshape(weight_shape)
    mode_params = pltpu.CompilerParams(vmem_limit_bytes=24 * 1024 * 1024)

    def mixing(kernel, value, name):
        return pl.pallas_call(
            kernel,
            out_shape=jax.ShapeDtypeStruct((owners, modes, lanes), f32),
            grid=grid,
            in_specs=[spectra_spec, weight_spec],
            out_specs=spectra_spec,
            compiler_params=mode_params,
            name=name,
        )(value, weight)

    mixture = exchange(mixing(mix_kernel, owned, "mix")).reshape(spectrum_shape)

    field = jax.ShapeDtypeStruct(field_shape, bf16)
    own, sent, slope_high, slope_low = pl.pallas_call(
        middle_kernel,
        out_shape=[spectrum, spectrum, field, field],
        grid_spec=pltpu.PrefetchScalarGridSpec(
            num_scalar_prefetch=1,
            grid=(1,),
            in_specs=[
                entire(spectrum_shape), entire(spectrum_shape), sample, sample, entire(pointwise_weight.shape),
                mine(x_inverse), mine(x_forward), mine(scaled_table), others(scaled_table),
            ],
            out_specs=[entire(spectrum_shape)] * 2 + [entire(field_shape)] * 2,
            scratch_shapes=u_scratch + t_scratch + [pltpu.VMEM(field_shape, f32)],
        ),
        compiler_params=params,
        name="middle",
    )(place, mixture, other_core(mixture), inputs, cotangent, pointwise_weight, x_inverse, x_forward, scaled_table, scaled_table)
    slopes = exchange((own + other_core(sent)).reshape(owners, modes, lanes))

    plane = pl.BlockSpec((1, channels, cells), lambda i: (i, 0, 0))
    local = pl.pallas_call(
        local_kernel,
        out_shape=jax.ShapeDtypeStruct(field_shape, f32),
        grid=(width,),
        in_specs=[plane, plane, pl.BlockSpec(pointwise_weight.shape, lambda i: (0, 0))],
        out_specs=plane,
        cost_estimate=pl.CostEstimate(flops=4 * 10**9, bytes_accessed=4 * 10**6, transcendentals=0),
        name="local",
    )(slope_high, slope_low, pointwise_weight)

    back = exchange(mixing(adjoint_kernel, slopes, "adjoint")).reshape(spectrum_shape)

    whole = jax.ShapeDtypeStruct(weight_shape, f32)
    new_weight, new_first, new_second = pl.pallas_call(
        adam_kernel,
        out_shape=[whole] * 3,
        grid=grid,
        in_specs=[spectra_spec, spectra_spec] + [weight_spec] * 3,
        out_specs=[weight_spec] * 3,
        compiler_params=mode_params,
        cost_estimate=pl.CostEstimate(flops=10**10, bytes_accessed=3 * 10**7, transcendentals=10**6),
        name="adam",
    )(owned, slopes, weight, first_moment.reshape(weight_shape), second_moment.reshape(weight_shape))

    out_field = pl.pallas_call(
        last_kernel,
        out_shape=jax.ShapeDtypeStruct(inputs.shape, bf16),
        grid_spec=pltpu.PrefetchScalarGridSpec(
            num_scalar_prefetch=1,
            grid=(1,),
            in_specs=[
                entire(spectrum_shape), entire(spectrum_shape), entire(field_shape),
                mine(x_inverse), mine(plain_table), others(plain_table),
            ],
            out_specs=sample,
            scratch_shapes=u_scratch + t_scratch,
        ),
        compiler_params=params,
        name="last",
    )(place, back, other_core(back), local, x_inverse, plain_table, plain_table)
    shape = spectral_weight.shape
    return (out_field, new_weight.reshape(shape), new_first.reshape(shape), new_second.reshape(shape))


def solution(mesh):
    return jax.shard_map(
        body,
        mesh=mesh,
        in_specs=(
            P(("grp", "dp"), "space", None, None),
            P(("grp", "dp"), "space", None, None),
            P(("grp", "space"), "dp", None, None, None),
            P(("grp", "space"), "dp", None, None, None),
            P(("grp", "space"), "dp", None, None, None),
            P("grp", None),
        ),
        out_specs=(
            P(("grp", "dp"), "space", None, None),
            P(("grp", "space"), "dp", None, None, None),
            P(("grp", "space"), "dp", None, None, None),
            P(("grp", "space"), "dp", None, None, None),
        ),
        check_vma=False,
    )
```

```python
import functools
import math

import jax
import jax.numpy as jnp
import ml_dtypes
import numpy as np
from jax import lax
from jax.experimental import pallas as pl
from jax.experimental.pallas import tpu as pltpu
from jax.sharding import PartitionSpec as P

MX = 16
MY = 16
MZ = 9
GX = 32
GY = 16
GZ = 32
HALF = MX // 2 + 1
CBLOCK = 16
ORDER = (0, 1, 2, 3, 4, 5, 6, 7)
BACK_ORDER = (4, 5, 6, 7, 3, 2, 1, 0)
LAST_ORDER = (1, 2, 4, 5, 6, 7, 3, 0)

beta_first = 0.9
beta_second = 0.999
learn_rate = 0.001
adam_epsilon = 1e-08
first_correct = 1.0 - math.exp(1000.0 * math.log(0.9))
second_correct = 1.0 - math.exp(1000.0 * math.log(0.999))

f32 = jnp.float32
bf16 = jnp.bfloat16


def split_np(table):
    high = table.astype(np.float32).astype(ml_dtypes.bfloat16)
    low = (table - high.astype(np.float64)).astype(np.float32).astype(ml_dtypes.bfloat16)
    return high, low


def yz_tables(groups, scaled):
    per_group = MY // groups
    y_frequency = np.concatenate([np.arange(MY // 2), np.arange(GY - MY // 2, GY)]).reshape(groups, per_group)
    y_place = np.repeat(np.arange(GY), GZ)
    z_place = np.tile(np.arange(GZ), GY)
    turns = y_frequency[:, :, None, None] * y_place / GY + np.arange(MZ)[None, None, :, None] * z_place / GZ
    angle = 2.0 * np.pi * (turns % 1.0)
    table = np.stack([np.cos(angle), -np.sin(angle)], axis=1)
    if scaled:
        table = table * (np.where(np.arange(MZ) == 0, 1.0, 2.0) / (GX * GY * GZ))[:, None]
    table = table.reshape(groups, 2 * per_group * MZ, GY * GZ)
    return np.concatenate(split_np(table), axis=1)


def x_tables(groups):
    width = GX // groups
    place = np.arange(GX).reshape(groups, 1, width)
    angle = 2.0 * np.pi * (np.arange(HALF)[None, :, None] * place % GX) / GX
    table = np.stack([np.cos(angle), -np.sin(angle)], axis=2).reshape(groups, 2 * HALF, width)
    wide = np.einsum("gkx,cd->gkcxd", table, np.eye(CBLOCK)).reshape(groups, 2 * HALF * CBLOCK, width * CBLOCK)
    high, low = split_np(wide)
    forward = np.concatenate([high, low, high], axis=2)
    flip = lambda t: np.swapaxes(t, 1, 2)
    inverse = np.concatenate([flip(high), flip(low), flip(high)], axis=2)
    return forward, np.ascontiguousarray(inverse)


def dot(a, b):
    return lax.dot_general(a, b, (((1,), (0,)), ((), ())), preferred_element_type=f32)


def dot_nt(a, b):
    return lax.dot_general(a, b, (((1,), (1,)), ((), ())), preferred_element_type=f32)


def dot_tn(a, b):
    return lax.dot_general(a, b, (((0,), (0,)), ((), ())), preferred_element_type=f32)


def split(value):
    high = value.astype(bf16)
    return high, (value - high.astype(f32)).astype(bf16)


def lane_sign(shape, first):
    lane = lax.broadcasted_iota(jnp.int32, shape, len(shape) - 1)
    return jnp.where(lane < shape[-1] // 2, first, -first).astype(f32)


def swap(value):
    return pltpu.roll(value, value.shape[-1] // 2, value.ndim - 1)


def to_spectra(channels, fields, x_table, own, other, own_out, other_out, u_high, u_low, ready=None):
    for block in range(channels // CBLOCK):
        pieces = fields(block)
        cells = pieces[0].shape[0]
        stacked = pieces[0] if len(pieces) == 1 else jnp.concatenate(pieces, axis=0)
        result = dot(x_table[:, : cells * len(pieces)], stacked)
        high, low = split(result)
        rows = pl.ds(block * CBLOCK, CBLOCK)
        shape = (2 * HALF, CBLOCK, high.shape[-1])
        u_high[:, rows, :] = high.reshape(shape)
        u_low[:, rows, :] = low.reshape(shape)
    if ready is not None:
        ready()
    table = jnp.concatenate([own[...], other[...]], axis=0)
    part = own.shape[0] // 2
    count = part // 2
    brief = jnp.concatenate([own[:part, :], other[:part, :]], axis=0)
    width = 2 * channels
    sign = lane_sign((count, width), -1.0)
    for first in range(0, HALF, 2):
        several = min(2, HALF - first)
        at = pl.ds(2 * first, 2 * several)
        high = u_high[at].reshape(several * width, u_high.shape[-1])
        low = u_low[at].reshape(several * width, u_low.shape[-1])
        wide = dot_nt(table, high)
        small = dot_nt(brief, low)
        for which, out in enumerate((own_out, other_out)):
            base = 2 * part * which
            total = (wide[base : base + part] + wide[base + part : base + 2 * part]) + small[
                part * which : part * (which + 1)
            ]
            for step in range(several):
                kx = first + step
                real = total[:count, step * width : (step + 1) * width]
                imag = swap(total[count:, step * width : (step + 1) * width])
                if kx < MX // 2:
                    out[kx] = real + imag * sign
                if kx > 0:
                    out[MX - kx] = imag - real * sign


def gather(place, order, sources, target):
    for step, source in zip(order, sources):
        block = source.shape[0]
        target[pl.ds((place[1] ^ step) * block, block)] = source[...]


def scatter(place, order, source, target):
    block = target.shape[1]
    for index, step in enumerate(order):
        target[index] = source[pl.ds((place[1] ^ step) * block, block)]


def from_spectra(channels, own_in, other_in, x_table, own, other, u_high, u_low, t_high, t_low):
    part = own.shape[0] // 2
    count = part // 2
    width = 2 * channels
    sign = lane_sign((count, width), -1.0)
    for kx in range(HALF):
        pieces = []
        for source in (own_in, other_in):
            if kx == 0:
                ahead = source[0]
                real, imag = ahead, ahead * sign
            elif kx == MX // 2:
                behind = source[MX - kx]
                real, imag = -behind * sign, behind
            else:
                ahead, behind = source[kx], source[MX - kx]
                real, imag = ahead - behind * sign, ahead * sign + behind
            pieces += [real, swap(imag)]
        turned = jnp.concatenate(pieces, axis=0).T
        high, low = split(turned)
        t_high[pl.ds(kx * width, width), :] = high
        t_low[pl.ds(kx * width, width), :] = low
    table_high = jnp.concatenate([own[:part, :], other[:part, :]], axis=0)
    table_low = jnp.concatenate([own[part:, :], other[part:, :]], axis=0)
    several = 3 if HALF % 3 == 0 else 1
    for first in range(0, HALF, several):
        at = pl.ds(first * width, several * width)
        high, low = t_high[at, :], t_low[at, :]
        value = dot(high, table_high) + dot(low, table_high) + dot(high, table_low)
        value_high, value_low = split(value)
        shape = (2 * several, channels, value.shape[-1])
        u_high[pl.ds(2 * first, 2 * several)] = value_high.reshape(shape)
        u_low[pl.ds(2 * first, 2 * several)] = value_low.reshape(shape)

    def block(index):
        rows = pl.ds(index * CBLOCK, CBLOCK)
        shape = (2 * HALF * CBLOCK, u_high.shape[-1])
        high = u_high[:, rows, :].reshape(shape)
        low = u_low[:, rows, :].reshape(shape)
        return dot(x_table[...], jnp.concatenate([high, high, low], axis=0))

    return block


def first_kernel(
    order, field_in, x_in, table_in, own_part, other_part, field, x_table, own, other, sems, u_high, u_low, own_out, other_out
):
    blocks, width, _, cells = field.shape
    space = lax.axis_index("space")
    place = (space, lax.axis_index("dp") if len(order) > 1 else 0)
    copies = [pltpu.make_async_copy(x_in.at[space], x_table, sems.at[0])]
    for block in range(blocks):
        piece = field_in.at[0, :, pl.ds(block * CBLOCK, CBLOCK), :]
        copies.append(pltpu.make_async_copy(piece, field.at[block], sems.at[1 + block]))
    copies.append(pltpu.make_async_copy(table_in.at[space], own, sems.at[1 + blocks]))
    copies.append(pltpu.make_async_copy(table_in.at[1 - space], other, sems.at[2 + blocks]))
    for copy in copies:
        copy.start()
    copies[0].wait()

    def fields(block):
        copies[1 + block].wait()
        piece = field[block].reshape(width * CBLOCK, cells)
        return [piece, piece]

    def ready():
        copies[1 + blocks].wait()
        copies[2 + blocks].wait()

    channels = blocks * CBLOCK
    to_spectra(channels, fields, x_table, own, other, own_out, other_out, u_high, u_low, ready)
    scatter(place, order, other_out, other_part)
    scatter(place, order, own_out, own_part)


def middle_kernel(back_order, order, place, *refs):
    number = len(back_order)
    own_blocks, other_blocks = refs[:number], refs[number : 2 * number]
    field, cotangent, pointwise, x_inverse, x_forward, own, other, *refs = refs[2 * number :]
    own_part, other_part, slope_high, slope_low, u_high, u_low, t_high, t_low, own_in, other_in, pre = refs
    gather(place, back_order, own_blocks, own_in)
    gather(place, back_order, other_blocks, other_in)
    width, channels, cells = field.shape
    block = from_spectra(channels, own_in, other_in, x_inverse, own, other, u_high, u_low, t_high, t_low)
    for index in range(channels // CBLOCK):
        pre[:, pl.ds(index * CBLOCK, CBLOCK), :] = block(index).reshape(width, CBLOCK, cells)
    root = math.sqrt(2.0 / math.pi)
    mixer = jnp.concatenate(split(pointwise[...].T), axis=0)

    @pl.loop(0, width)
    def _(x):
        local = dot(mixer, field[x])
        value = pre[x] + (local[:channels] + local[channels:])
        square = value * value
        tanh = jnp.tanh(root * value * (1.0 + 0.044715 * square))
        slope = 0.5 * (1.0 + tanh) + (0.5 * root) * value * (1.0 - tanh * tanh) * (1.0 + 3.0 * 0.044715 * square)
        slope = slope * cotangent[x].astype(f32)
        high, low = split(slope)
        slope_high[x] = high
        slope_low[x] = low

    def fields(index):
        rows = pl.ds(index * CBLOCK, CBLOCK)
        shape = (width * CBLOCK, cells)
        high = slope_high[:, rows, :].reshape(shape)
        return [high, high, slope_low[:, rows, :].reshape(shape)]

    to_spectra(channels, fields, x_forward, own, other, own_in, other_in, u_high, u_low)
    scatter(place, order, other_in, other_part)
    scatter(place, order, own_in, own_part)


def last_kernel(order, place, *refs):
    number = len(order)
    own_blocks, other_blocks = refs[:number], refs[number : 2 * number]
    local, x_inverse, own, other, out, u_high, u_low, t_high, t_low, own_in, other_in = refs[2 * number :]
    gather(place, order, own_blocks, own_in)
    gather(place, order, other_blocks, other_in)
    width, channels, cells = out.shape
    block = from_spectra(channels, own_in, other_in, x_inverse, own, other, u_high, u_low, t_high, t_low)
    for index in range(channels // CBLOCK):
        rows = pl.ds(index * CBLOCK, CBLOCK)
        value = block(index).reshape(width, CBLOCK, cells) + local[:, rows, :]
        out[:, rows, :] = value.astype(bf16)


def local_gradient(high_in, low_in, pointwise, out):
    channels = pointwise.shape[0]
    high, low = split(pointwise[...])
    both = jnp.concatenate([high, low], axis=0)

    @pl.loop(0, out.shape[0])
    def _(x):
        wide = dot(both, high_in[x])
        out[x] = (wide[:channels] + wide[channels:]) + dot(high, low_in[x])


def pairs_of(count):
    return [list(range(first, min(first + 2, count))) for first in range(0, count, 2)]


def spread_rows(rows, lower):
    if len(rows) == 1:
        half = rows[0].shape[-1] // 2
        return jnp.concatenate([rows[0][:, :half], rows[0][:, half:]], axis=0)
    zero = jnp.zeros_like(rows[0])
    one, two = rows
    return jnp.concatenate(
        [
            jnp.where(lower, one, zero),
            jnp.where(lower, swap(one), zero),
            jnp.where(lower, zero, swap(two)),
            jnp.where(lower, zero, two),
        ],
        axis=0,
    )


def lower_half(shape):
    return lax.broadcasted_iota(jnp.int32, shape, 1) < shape[1] // 2


def mode_chunk(modes):
    return 16 if modes % 16 == 0 else modes


def stack(refs, target):
    base = 0
    for ref in refs:
        target[pl.ds(base, ref.shape[0])] = ref[...]
        base += ref.shape[0]


def unstack(source, refs):
    base = 0
    for ref in refs:
        ref[...] = source[pl.ds(base, ref.shape[0])]
        base += ref.shape[0]


def split_kernel(weight, high, low):
    high[...], low[...] = split(weight[...])


def local_split_kernel(slope_high, slope_low, pointwise, weight, local, high, low):
    local_gradient(slope_high, slope_low, pointwise, local)
    modes = weight.shape[0]
    chunk = mode_chunk(modes)

    @pl.loop(0, modes // chunk)
    def _(index):
        at = pl.ds(index * chunk, chunk)
        high[at], low[at] = split(weight[at])


def hold_kernel(*refs):
    number = len(refs) // 2
    for source, target in zip(refs[:number], refs[number:]):
        target[...] = source[...]


def mode_kernel(one_chunk, number, *refs):
    sources, weights, refs = refs[:number], refs[number : number + 2], refs[number + 2 :]
    spectra, out = refs[-2:]
    stack(sources, spectra)
    modes = spectra.shape[1]
    chunk = mode_chunk(modes)

    @pl.loop(0, modes // chunk)
    def _(index):
        start = index * chunk
        rows = [spectra[:, start + mode, :] for mode in range(chunk)]

        def weight(first, count):
            values = [part[pl.ds(start + first, count)] for part in weights]
            return [value.reshape(-1, value.shape[-1]) for value in values]

        for mode, value in enumerate(one_chunk(rows, weight)):
            out[:, start + mode, :] = value

    unstack(out, refs[:number])


def mix_chunk(rows_of, weight):
    samples, width = rows_of[0].shape
    lower = lower_half((samples, width))
    sign = lane_sign((samples, width), -1.0)
    results = []
    for group in pairs_of(len(rows_of)):
        rows = spread_rows([rows_of[mode] for mode in group], lower)
        high, low = split(rows)
        block_high, block_low = weight(group[0], len(group))
        wide = dot(jnp.concatenate([high, low], axis=0), block_high)
        total = wide[: rows.shape[0]] + wide[rows.shape[0] :] + dot(high, block_low)
        for step, mode in enumerate(group):
            base = 2 * samples * step
            real, imag = total[base : base + samples], total[base + samples : base + 2 * samples]
            results.append(real + swap(imag) * sign)
    return results


def adjoint_chunk(rows_of, weight):
    samples, width = rows_of[0].shape
    lower = lower_half((samples, width))
    sign = lane_sign((samples, width), 1.0)
    results = []
    for group in pairs_of(len(rows_of)):
        rows = []
        for mode in group:
            rows += [rows_of[mode], swap(rows_of[mode]) * sign]
        rows = jnp.concatenate(rows, axis=0)
        high, low = split(rows)
        block_high, block_low = weight(group[0], len(group))
        wide = dot_nt(jnp.concatenate([high, low], axis=0), block_high)
        total = wide[: rows.shape[0]] + wide[rows.shape[0] :] + dot_nt(high, block_low)
        for step in range(len(group)):
            base = 2 * samples * step
            real, imag = total[base : base + samples], total[base + samples : base + 2 * samples]
            if len(group) == 1:
                results.append(jnp.concatenate([real, imag], axis=1))
            elif step == 0:
                results.append(jnp.where(lower, real, swap(imag)))
            else:
                results.append(jnp.where(lower, swap(real), imag))
    return results


def adam_kernel(number, *refs):
    spectra_parts, slope_parts, refs = refs[:number], refs[number : 2 * number], refs[2 * number :]
    weight, first, second, weight_out, first_out, second_out, spectra, slopes = refs
    stack(spectra_parts, spectra)
    stack(slope_parts, slopes)
    samples, modes, width = spectra.shape
    lower = lower_half((samples, width))
    sign = lane_sign((samples, width), 1.0)
    for group in pairs_of(modes):
        left = spread_rows([spectra[:, mode, :] for mode in group], lower)
        right = []
        for mode in group:
            row = slopes[:, mode, :]
            right += [row, swap(row) * sign]
        right = jnp.concatenate(right, axis=0)
        left_high, left_low = split(left)
        right_high, right_low = split(right)
        gradient = dot_tn(
            jnp.concatenate([left_high, left_low, left_high], axis=0),
            jnp.concatenate([right_high, right_high, right_low], axis=0),
        )
        at = pl.ds(group[0], len(group))
        shape = (len(group),) + weight.shape[1:]
        gradient = gradient.reshape(shape)
        new_first = beta_first * first[at] + (1.0 - beta_first) * gradient
        new_second = beta_second * second[at] + (1.0 - beta_second) * gradient * gradient
        bottom = jnp.sqrt(new_second * (1.0 / second_correct)) + adam_epsilon
        first_out[at] = new_first
        second_out[at] = new_second
        weight_out[at] = weight[at] - (learn_rate / first_correct) * new_first / bottom


def body(inputs, cotangent, spectral_weight, first_moment, second_moment, pointwise_weight):
    groups = lax.axis_size("space")
    owners = lax.axis_size("dp")
    assert groups == 2 and inputs.shape[0] == 1
    per_group = MY // groups
    _, width, channels, cells = inputs.shape
    lanes = 2 * channels
    count = per_group * MZ
    pairs = spectral_weight.shape[1]
    modes = pairs * MZ
    paired = owners in (2, 4, 8)
    order, back_order, last_order = (
        [step for step in steps if step < owners] if paired else [0] for steps in (ORDER, BACK_ORDER, LAST_ORDER)
    )
    blocks = owners if paired else 1
    owner = lax.axis_index("dp").astype(jnp.int32)
    place = jnp.stack([lax.axis_index("space").astype(jnp.int32), owner if paired else jnp.int32(0)])

    plain_table = jnp.asarray(yz_tables(groups, False))
    scaled_table = jnp.asarray(yz_tables(groups, True))
    x_forward, x_inverse = x_tables(groups)
    x_brief = jnp.asarray(x_forward[:, :, : 2 * width * CBLOCK])
    x_forward, x_inverse = jnp.asarray(x_forward), jnp.asarray(x_inverse)

    def mine(array):
        return pl.BlockSpec((None,) + array.shape[1:], lambda i, s: (s[0], 0, 0))

    def others(array):
        return pl.BlockSpec((None,) + array.shape[1:], lambda i, s: (1 - s[0], 0, 0))

    def entire(shape):
        return pl.BlockSpec(shape, lambda i, s: (0,) * len(shape))

    sample = pl.BlockSpec((None, width, channels, cells), lambda i, s: (0, 0, 0, 0))
    spectrum_shape = (MX, count, lanes)
    spectrum = jax.ShapeDtypeStruct(spectrum_shape, f32)
    field_shape = (width, channels, cells)
    u_scratch = [pltpu.VMEM((2 * HALF, channels, cells), bf16)] * 2
    t_scratch = [pltpu.VMEM((HALF * lanes, 2 * groups * count), bf16)] * 2
    params = pltpu.CompilerParams(vmem_limit_bytes=20 * 1024 * 1024)

    def other_core(value):
        return lax.ppermute(value, "space", [(0, 1), (1, 0)])

    spectrum_scratch = [pltpu.VMEM(spectrum_shape, f32)] * 2
    part_shape = (blocks, MX // blocks, count, lanes)
    block_specs = [entire(part_shape[1:])] * (2 * blocks)
    part_type = jax.ShapeDtypeStruct(part_shape, f32)
    table_scratch = pltpu.VMEM(plain_table.shape[1:], bf16)
    own, sent = pl.pallas_call(
        functools.partial(first_kernel, order),
        out_shape=[part_type] * 2,
        in_specs=[pl.BlockSpec(memory_space=pltpu.HBM)] * 3,
        scratch_shapes=[
            pltpu.VMEM((channels // CBLOCK, width, CBLOCK, cells), bf16),
            pltpu.VMEM(x_brief.shape[1:], bf16),
            table_scratch,
            table_scratch,
            pltpu.SemaphoreType.DMA((channels // CBLOCK + 3,)),
        ]
        + u_scratch
        + spectrum_scratch,
        compiler_params=pltpu.CompilerParams(vmem_limit_bytes=62 * 1024 * 1024),
        name="first",
    )(inputs, x_brief, plain_table)

    weight_shape = (modes, channels, lanes)
    weight, own = lax.optimization_barrier((spectral_weight.reshape(weight_shape), own))

    def travel(value, step):
        return lax.ppermute(value, "dp", [(i, i ^ step) for i in range(owners)]) if step else value

    def to_owners(own, sent):
        got = other_core(sent)
        if not paired:
            return [lax.all_to_all((own + got).reshape(owners, modes, lanes), "dp", 0, 0, tiled=True)]
        return [travel((own[i] + got[i]).reshape(1, modes, lanes), step) for i, step in enumerate(order)]

    def from_owners(values, steps, tie=None):
        if not paired:
            values = [lax.all_to_all(values[0], "dp", 0, 0, tiled=True)]
        else:
            values = [travel(values[order.index(step)], step) for step in steps]
        if tie is not None:
            values, tie = lax.optimization_barrier((values, tie))
        values = [value.reshape(part_shape[1:]) for value in values]
        return values + [other_core(value) for value in values], tie

    mode_params = pltpu.CompilerParams(vmem_limit_bytes=14 * 1024 * 1024)

    def estimate(microseconds):
        return pl.CostEstimate(flops=microseconds * 10**9, bytes_accessed=10**5, transcendentals=0)

    def mixing(chunk, values, weights, name):
        return pl.pallas_call(
            functools.partial(mode_kernel, chunk, len(values)),
            out_shape=[jax.ShapeDtypeStruct(value.shape, f32) for value in values],
            scratch_shapes=[pltpu.VMEM((owners, modes, lanes), f32)] * 2,
            compiler_params=mode_params,
            cost_estimate=estimate(1),
            name=name,
        )(*values, *weights)

    large = 48 if modes % 48 == 0 else modes
    large_spec = pl.BlockSpec((large, channels, lanes), lambda i: (i, 0, 0))
    def split_weights(weight):
        return pl.pallas_call(
            split_kernel,
            out_shape=[jax.ShapeDtypeStruct(weight_shape, bf16)] * 2,
            grid=(modes // large,),
            in_specs=[large_spec],
            out_specs=[large_spec] * 2,
            compiler_params=mode_params,
            cost_estimate=estimate(6),
            name="split",
        )(weight)

    def hold(*values):
        return pl.pallas_call(
            hold_kernel,
            out_shape=[jax.ShapeDtypeStruct(value.shape, value.dtype) for value in values],
            compiler_params=mode_params,
            cost_estimate=estimate(6),
            name="hold",
        )(*values)

    owned = to_owners(own, sent)
    mixture = list(mixing(mix_chunk, owned, split_weights(weight), "mix"))
    mixture[0], field_in, cotangent = lax.optimization_barrier((mixture[0], inputs, cotangent))
    held = hold(field_in, cotangent, x_inverse, x_forward, scaled_table)
    mixed, held = from_owners(mixture, back_order, held)

    field = jax.ShapeDtypeStruct(field_shape, bf16)
    own, sent, slope_high, slope_low = pl.pallas_call(
        functools.partial(middle_kernel, back_order, order),
        out_shape=[part_type] * 2 + [field, field],
        grid_spec=pltpu.PrefetchScalarGridSpec(
            num_scalar_prefetch=1,
            grid=(1,),
            in_specs=[
                *block_specs, sample, sample, entire(pointwise_weight.shape),
                mine(x_inverse), mine(x_forward), mine(scaled_table), others(scaled_table),
            ],
            out_specs=[entire(part_shape)] * 2 + [entire(field_shape)] * 2,
            scratch_shapes=u_scratch + t_scratch + spectrum_scratch + [pltpu.VMEM(field_shape, f32)],
        ),
        compiler_params=params,
        name="middle",
    )(place, *mixed, *held[:2], pointwise_weight, *held[2:], held[4])
    again, own = lax.optimization_barrier((weight, own))
    slopes = to_owners(own, sent)
    local, *weights = pl.pallas_call(
        local_split_kernel,
        out_shape=[jax.ShapeDtypeStruct(field_shape, f32)] + [jax.ShapeDtypeStruct(weight_shape, bf16)] * 2,
        cost_estimate=estimate(6),
        compiler_params=mode_params,
        name="local",
    )(slope_high, slope_low, pointwise_weight, again)
    turned = mixing(adjoint_chunk, slopes, weights, "adjoint")

    block = 24 if modes % 24 == 0 else modes
    whole = jax.ShapeDtypeStruct(weight_shape, f32)
    weight_spec = pl.BlockSpec((block, channels, lanes), lambda i: (i, 0, 0))
    value_specs = [pl.BlockSpec((value.shape[0], block, lanes), lambda i: (0, i, 0)) for value in owned]
    new_weight, new_first, new_second = pl.pallas_call(
        functools.partial(adam_kernel, len(owned)),
        out_shape=[whole] * 3,
        grid=(modes // block,),
        in_specs=value_specs * 2 + [weight_spec] * 3,
        out_specs=[weight_spec] * 3,
        scratch_shapes=[pltpu.VMEM((owners, block, lanes), f32)] * 2,
        compiler_params=pltpu.CompilerParams(vmem_limit_bytes=56 * 1024 * 1024),
        cost_estimate=pl.CostEstimate(flops=10**10, bytes_accessed=3 * 10**7, transcendentals=10**6),
        name="adam",
    )(*owned, *slopes, weight, first_moment.reshape(weight_shape), second_moment.reshape(weight_shape))
    mixed, new_first = from_owners(turned, last_order, new_first)

    out_field = pl.pallas_call(
        functools.partial(last_kernel, last_order),
        out_shape=jax.ShapeDtypeStruct(inputs.shape, bf16),
        grid_spec=pltpu.PrefetchScalarGridSpec(
            num_scalar_prefetch=1,
            grid=(1,),
            in_specs=[*block_specs, entire(field_shape), mine(x_inverse), mine(plain_table), others(plain_table)],
            out_specs=sample,
            scratch_shapes=u_scratch + t_scratch + spectrum_scratch,
        ),
        compiler_params=params,
        name="last",
    )(place, *mixed, local, x_inverse, plain_table, plain_table)
    shape = spectral_weight.shape
    return (out_field, new_weight.reshape(shape), new_first.reshape(shape), new_second.reshape(shape))


def solution(mesh):
    return jax.shard_map(
        body,
        mesh=mesh,
        in_specs=(
            P(("grp", "dp"), "space", None, None),
            P(("grp", "dp"), "space", None, None),
            P(("grp", "space"), "dp", None, None, None),
            P(("grp", "space"), "dp", None, None, None),
            P(("grp", "space"), "dp", None, None, None),
            P("grp", None),
        ),
        out_specs=(
            P(("grp", "dp"), "space", None, None),
            P(("grp", "space"), "dp", None, None, None),
            P(("grp", "space"), "dp", None, None, None),
            P(("grp", "space"), "dp", None, None, None),
        ),
        check_vma=False,
    )
```

```python
import functools
import math

import jax
import jax.numpy as jnp
import ml_dtypes
import numpy as np
from jax import lax
from jax.experimental import pallas as pl
from jax.experimental.pallas import tpu as pltpu
from jax.sharding import PartitionSpec as P

MX = 16
MY = 16
MZ = 9
GX = 32
GY = 16
GZ = 32
HALF = MX // 2 + 1
CBLOCK = 16
ORDER = (0, 1, 2, 3, 4, 5, 6, 7)
BACK_ORDER = (4, 5, 6, 7, 3, 2, 1, 0)
LAST_ORDER = (1, 2, 4, 5, 6, 7, 3, 0)

beta_first = 0.9
beta_second = 0.999
learn_rate = 0.001
adam_epsilon = 1e-08
first_correct = 1.0 - math.exp(1000.0 * math.log(0.9))
second_correct = 1.0 - math.exp(1000.0 * math.log(0.999))

f32 = jnp.float32
bf16 = jnp.bfloat16


def split_np(table):
    high = table.astype(np.float32).astype(ml_dtypes.bfloat16)
    low = (table - high.astype(np.float64)).astype(np.float32).astype(ml_dtypes.bfloat16)
    return high, low


def yz_tables(groups, scaled):
    per_group = MY // groups
    y_frequency = np.concatenate([np.arange(MY // 2), np.arange(GY - MY // 2, GY)]).reshape(groups, per_group)
    y_place = np.repeat(np.arange(GY), GZ)
    z_place = np.tile(np.arange(GZ), GY)
    turns = y_frequency[:, :, None, None] * y_place / GY + np.arange(MZ)[None, None, :, None] * z_place / GZ
    angle = 2.0 * np.pi * (turns % 1.0)
    table = np.stack([np.cos(angle), -np.sin(angle)], axis=1)
    if scaled:
        table = table * (np.where(np.arange(MZ) == 0, 1.0, 2.0) / (GX * GY * GZ))[:, None]
    table = table.reshape(groups, 2 * per_group * MZ, GY * GZ)
    return np.concatenate(split_np(table), axis=1)


def x_tables(groups):
    width = GX // groups
    place = np.arange(GX).reshape(groups, 1, width)
    angle = 2.0 * np.pi * (np.arange(HALF)[None, :, None] * place % GX) / GX
    table = np.stack([np.cos(angle), -np.sin(angle)], axis=2).reshape(groups, 2 * HALF, width)
    wide = np.einsum("gkx,cd->gkcxd", table, np.eye(CBLOCK)).reshape(groups, 2 * HALF * CBLOCK, width * CBLOCK)
    high, low = split_np(wide)
    forward = np.concatenate([high, low, high], axis=2)
    flip = lambda t: np.swapaxes(t, 1, 2)
    inverse = np.concatenate([flip(high), flip(low), flip(high)], axis=2)
    return forward, np.ascontiguousarray(inverse)


def dot(a, b):
    return lax.dot_general(a, b, (((1,), (0,)), ((), ())), preferred_element_type=f32)


def dot_nt(a, b):
    return lax.dot_general(a, b, (((1,), (1,)), ((), ())), preferred_element_type=f32)


def dot_tn(a, b):
    return lax.dot_general(a, b, (((0,), (0,)), ((), ())), preferred_element_type=f32)


def split(value):
    high = value.astype(bf16)
    return high, (value - high.astype(f32)).astype(bf16)


def lane_sign(shape, first):
    lane = lax.broadcasted_iota(jnp.int32, shape, len(shape) - 1)
    return jnp.where(lane < shape[-1] // 2, first, -first).astype(f32)


def swap(value):
    return pltpu.roll(value, value.shape[-1] // 2, value.ndim - 1)


def to_spectra(channels, fields, x_table, own, other, own_out, other_out, u_high, u_low, ready=None):
    for block in range(channels // CBLOCK):
        pieces = fields(block)
        cells = pieces[0].shape[0]
        stacked = pieces[0] if len(pieces) == 1 else jnp.concatenate(pieces, axis=0)
        result = dot(x_table[:, : cells * len(pieces)], stacked)
        high, low = split(result)
        rows = pl.ds(block * CBLOCK, CBLOCK)
        shape = (2 * HALF, CBLOCK, high.shape[-1])
        u_high[:, rows, :] = high.reshape(shape)
        u_low[:, rows, :] = low.reshape(shape)
    if ready is not None:
        ready()
    table = jnp.concatenate([own[...], other[...]], axis=0)
    part = own.shape[0] // 2
    count = part // 2
    brief = jnp.concatenate([own[:part, :], other[:part, :]], axis=0)
    width = 2 * channels
    sign = lane_sign((count, width), -1.0)
    for first in range(0, HALF, 2):
        several = min(2, HALF - first)
        at = pl.ds(2 * first, 2 * several)
        high = u_high[at].reshape(several * width, u_high.shape[-1])
        low = u_low[at].reshape(several * width, u_low.shape[-1])
        wide = dot_nt(table, high)
        small = dot_nt(brief, low)
        for which, out in enumerate((own_out, other_out)):
            base = 2 * part * which
            total = (wide[base : base + part] + wide[base + part : base + 2 * part]) + small[
                part * which : part * (which + 1)
            ]
            for step in range(several):
                kx = first + step
                real = total[:count, step * width : (step + 1) * width]
                imag = swap(total[count:, step * width : (step + 1) * width])
                if kx < MX // 2:
                    out[kx] = real + imag * sign
                if kx > 0:
                    out[MX - kx] = imag - real * sign


def gather(place, order, sources, target):
    for step, source in zip(order, sources):
        block = source.shape[0]
        target[pl.ds((place[1] ^ step) * block, block)] = source[...]


def scatter(place, order, source, target):
    block = target.shape[1]
    for index, step in enumerate(order):
        target[index] = source[pl.ds((place[1] ^ step) * block, block)]


def from_spectra(channels, own_in, other_in, x_table, own, other, u_high, u_low, t_high, t_low):
    part = own.shape[0] // 2
    count = part // 2
    width = 2 * channels
    sign = lane_sign((count, width), -1.0)
    for kx in range(HALF):
        pieces = []
        for source in (own_in, other_in):
            if kx == 0:
                ahead = source[0]
                real, imag = ahead, ahead * sign
            elif kx == MX // 2:
                behind = source[MX - kx]
                real, imag = -behind * sign, behind
            else:
                ahead, behind = source[kx], source[MX - kx]
                real, imag = ahead - behind * sign, ahead * sign + behind
            pieces += [real, swap(imag)]
        turned = jnp.concatenate(pieces, axis=0).T
        high, low = split(turned)
        t_high[pl.ds(kx * width, width), :] = high
        t_low[pl.ds(kx * width, width), :] = low
    table_high = jnp.concatenate([own[:part, :], other[:part, :]], axis=0)
    table_low = jnp.concatenate([own[part:, :], other[part:, :]], axis=0)
    several = 3 if HALF % 3 == 0 else 1
    for first in range(0, HALF, several):
        at = pl.ds(first * width, several * width)
        high, low = t_high[at, :], t_low[at, :]
        value = dot(high, table_high) + dot(low, table_high) + dot(high, table_low)
        value_high, value_low = split(value)
        shape = (2 * several, channels, value.shape[-1])
        u_high[pl.ds(2 * first, 2 * several)] = value_high.reshape(shape)
        u_low[pl.ds(2 * first, 2 * several)] = value_low.reshape(shape)

    def block(index):
        rows = pl.ds(index * CBLOCK, CBLOCK)
        shape = (2 * HALF * CBLOCK, u_high.shape[-1])
        high = u_high[:, rows, :].reshape(shape)
        low = u_low[:, rows, :].reshape(shape)
        return dot(x_table[...], jnp.concatenate([high, high, low], axis=0))

    return block


def first_kernel(
    order, field_in, x_in, table_in, own_part, other_part, field, x_table, own, other, sems, u_high, u_low, own_out, other_out
):
    blocks, width, _, cells = field.shape
    space = lax.axis_index("space")
    place = (space, lax.axis_index("dp") if len(order) > 1 else 0)
    copies = [pltpu.make_async_copy(x_in.at[space], x_table, sems.at[0])]
    for block in range(blocks):
        piece = field_in.at[0, :, pl.ds(block * CBLOCK, CBLOCK), :]
        copies.append(pltpu.make_async_copy(piece, field.at[block], sems.at[1 + block]))
    copies.append(pltpu.make_async_copy(table_in.at[space], own, sems.at[1 + blocks]))
    copies.append(pltpu.make_async_copy(table_in.at[1 - space], other, sems.at[2 + blocks]))
    for copy in copies:
        copy.start()
    copies[0].wait()

    def fields(block):
        copies[1 + block].wait()
        piece = field[block].reshape(width * CBLOCK, cells)
        return [piece, piece]

    def ready():
        copies[1 + blocks].wait()
        copies[2 + blocks].wait()

    channels = blocks * CBLOCK
    to_spectra(channels, fields, x_table, own, other, own_out, other_out, u_high, u_low, ready)
    scatter(place, order, other_out, other_part)
    scatter(place, order, own_out, own_part)


def middle_kernel(back_order, order, place, *refs):
    number = len(back_order)
    own_blocks, other_blocks = refs[:number], refs[number : 2 * number]
    field, cotangent, pointwise, x_inverse, x_forward, own, other, *refs = refs[2 * number :]
    own_part, other_part, slope_high, slope_low, u_high, u_low, t_high, t_low, own_in, other_in, pre = refs
    gather(place, back_order, own_blocks, own_in)
    gather(place, back_order, other_blocks, other_in)
    width, channels, cells = field.shape
    block = from_spectra(channels, own_in, other_in, x_inverse, own, other, u_high, u_low, t_high, t_low)
    for index in range(channels // CBLOCK):
        pre[:, pl.ds(index * CBLOCK, CBLOCK), :] = block(index).reshape(width, CBLOCK, cells)
    root = math.sqrt(2.0 / math.pi)
    mixer = jnp.concatenate(split(pointwise[...].T), axis=0)

    @pl.loop(0, width, unroll=4)
    def _(x):
        local = dot(mixer, field[x])
        value = pre[x] + (local[:channels] + local[channels:])
        square = value * value
        tanh = jnp.tanh(root * value * (1.0 + 0.044715 * square))
        slope = 0.5 * (1.0 + tanh) + (0.5 * root) * value * (1.0 - tanh * tanh) * (1.0 + 3.0 * 0.044715 * square)
        slope = slope * cotangent[x].astype(f32)
        high, low = split(slope)
        slope_high[x] = high
        slope_low[x] = low

    def fields(index):
        rows = pl.ds(index * CBLOCK, CBLOCK)
        shape = (width * CBLOCK, cells)
        high = slope_high[:, rows, :].reshape(shape)
        return [high, high, slope_low[:, rows, :].reshape(shape)]

    to_spectra(channels, fields, x_forward, own, other, own_in, other_in, u_high, u_low)
    scatter(place, order, other_in, other_part)
    scatter(place, order, own_in, own_part)


def last_kernel(order, place, *refs):
    number = len(order)
    own_blocks, other_blocks = refs[:number], refs[number : 2 * number]
    local, x_inverse, own, other, out, u_high, u_low, t_high, t_low, own_in, other_in = refs[2 * number :]
    gather(place, order, own_blocks, own_in)
    gather(place, order, other_blocks, other_in)
    width, channels, cells = out.shape
    block = from_spectra(channels, own_in, other_in, x_inverse, own, other, u_high, u_low, t_high, t_low)
    for index in range(channels // CBLOCK):
        rows = pl.ds(index * CBLOCK, CBLOCK)
        value = block(index).reshape(width, CBLOCK, cells) + local[:, rows, :]
        out[:, rows, :] = value.astype(bf16)


def local_gradient(high_in, low_in, pointwise, out):
    channels = pointwise.shape[0]
    high, low = split(pointwise[...])
    both = jnp.concatenate([high, low], axis=0)

    @pl.loop(0, out.shape[0], unroll=4)
    def _(x):
        wide = dot(both, high_in[x])
        out[x] = (wide[:channels] + wide[channels:]) + dot(high, low_in[x])


def pairs_of(count):
    return [list(range(first, min(first + 2, count))) for first in range(0, count, 2)]


def spread_rows(rows, lower):
    if len(rows) == 1:
        half = rows[0].shape[-1] // 2
        return jnp.concatenate([rows[0][:, :half], rows[0][:, half:]], axis=0)
    zero = jnp.zeros_like(rows[0])
    one, two = rows
    return jnp.concatenate(
        [
            jnp.where(lower, one, zero),
            jnp.where(lower, swap(one), zero),
            jnp.where(lower, zero, swap(two)),
            jnp.where(lower, zero, two),
        ],
        axis=0,
    )


def lower_half(shape):
    return lax.broadcasted_iota(jnp.int32, shape, 1) < shape[1] // 2


def mode_chunk(modes):
    return 72 if modes % 72 == 0 else modes


def stack(refs, target):
    base = 0
    for ref in refs:
        target[pl.ds(base, ref.shape[0])] = ref[...]
        base += ref.shape[0]


def unstack(source, refs):
    base = 0
    for ref in refs:
        ref[...] = source[pl.ds(base, ref.shape[0])]
        base += ref.shape[0]


def split_kernel(weight, high, low):
    high[...], low[...] = split(weight[...])


def local_split_kernel(slope_high, slope_low, pointwise, weight, local, high, low):
    local_gradient(slope_high, slope_low, pointwise, local)
    modes = weight.shape[0]
    chunk = mode_chunk(modes)

    @pl.loop(0, modes // chunk)
    def _(index):
        at = pl.ds(index * chunk, chunk)
        high[at], low[at] = split(weight[at])


def hold_kernel(field, cotangent, x_inverse, x_forward, table, *targets):
    space = lax.axis_index("space")
    values = [field[0], cotangent[0], x_inverse[space], x_forward[space], table[space], table[1 - space]]
    for target, value in zip(targets, values):
        target[...] = value


def mode_kernel(one_chunk, number, *refs):
    sources, weights, refs = refs[:number], refs[number : number + 2], refs[number + 2 :]
    spectra, out = refs[-2:]
    stack(sources, spectra)
    modes = spectra.shape[1]
    chunk = mode_chunk(modes)

    @pl.loop(0, modes // chunk)
    def _(index):
        start = index * chunk
        rows = [spectra[:, start + mode, :] for mode in range(chunk)]

        def weight(first, count):
            values = [part[pl.ds(start + first, count)] for part in weights]
            return [value.reshape(-1, value.shape[-1]) for value in values]

        for mode, value in enumerate(one_chunk(rows, weight)):
            out[:, start + mode, :] = value

    unstack(out, refs[:number])


def mix_chunk(rows_of, weight):
    samples, width = rows_of[0].shape
    lower = lower_half((samples, width))
    sign = lane_sign((samples, width), -1.0)
    results = []
    for group in pairs_of(len(rows_of)):
        rows = spread_rows([rows_of[mode] for mode in group], lower)
        high, low = split(rows)
        block_high, block_low = weight(group[0], len(group))
        wide = dot(jnp.concatenate([high, low], axis=0), block_high)
        total = wide[: rows.shape[0]] + wide[rows.shape[0] :] + dot(high, block_low)
        for step, mode in enumerate(group):
            base = 2 * samples * step
            real, imag = total[base : base + samples], total[base + samples : base + 2 * samples]
            results.append(real + swap(imag) * sign)
    return results


def adjoint_chunk(rows_of, weight):
    samples, width = rows_of[0].shape
    lower = lower_half((samples, width))
    sign = lane_sign((samples, width), 1.0)
    results = []
    for group in pairs_of(len(rows_of)):
        rows = []
        for mode in group:
            rows += [rows_of[mode], swap(rows_of[mode]) * sign]
        rows = jnp.concatenate(rows, axis=0)
        high, low = split(rows)
        block_high, block_low = weight(group[0], len(group))
        wide = dot_nt(jnp.concatenate([high, low], axis=0), block_high)
        total = wide[: rows.shape[0]] + wide[rows.shape[0] :] + dot_nt(high, block_low)
        for step in range(len(group)):
            base = 2 * samples * step
            real, imag = total[base : base + samples], total[base + samples : base + 2 * samples]
            if len(group) == 1:
                results.append(jnp.concatenate([real, imag], axis=1))
            elif step == 0:
                results.append(jnp.where(lower, real, swap(imag)))
            else:
                results.append(jnp.where(lower, swap(real), imag))
    return results


def adam_kernel(number, *refs):
    spectra_parts, slope_parts, refs = refs[:number], refs[number : 2 * number], refs[2 * number :]
    weight, first, second, weight_out, first_out, second_out, spectra, slopes = refs
    samples, modes, width = spectra.shape
    here = pl.ds(pl.multiple_of(pl.program_id(0) * modes, 8) if modes % 8 == 0 else 0, modes)
    for parts, target in ((spectra_parts, spectra), (slope_parts, slopes)):
        base = 0
        for part in parts:
            target[pl.ds(base, part.shape[0])] = part[:, here, :]
            base += part.shape[0]
    lower = lower_half((samples, width))
    sign = lane_sign((samples, width), 1.0)
    for group in pairs_of(modes):
        left = spread_rows([spectra[:, mode, :] for mode in group], lower)
        right = []
        for mode in group:
            row = slopes[:, mode, :]
            right += [row, swap(row) * sign]
        right = jnp.concatenate(right, axis=0)
        left_high, left_low = split(left)
        right_high, right_low = split(right)
        gradient = dot_tn(
            jnp.concatenate([left_high, left_low, left_high], axis=0),
            jnp.concatenate([right_high, right_high, right_low], axis=0),
        )
        at = pl.ds(group[0], len(group))
        shape = (len(group),) + weight.shape[1:]
        gradient = gradient.reshape(shape)
        new_first = beta_first * first[at] + (1.0 - beta_first) * gradient
        new_second = beta_second * second[at] + (1.0 - beta_second) * gradient * gradient
        bottom = jnp.sqrt(new_second * (1.0 / second_correct)) + adam_epsilon
        first_out[at] = new_first
        second_out[at] = new_second
        weight_out[at] = weight[at] - (learn_rate / first_correct) * new_first / bottom


def body(inputs, cotangent, spectral_weight, first_moment, second_moment, pointwise_weight):
    groups = lax.axis_size("space")
    owners = lax.axis_size("dp")
    assert groups == 2 and inputs.shape[0] == 1
    per_group = MY // groups
    _, width, channels, cells = inputs.shape
    lanes = 2 * channels
    count = per_group * MZ
    pairs = spectral_weight.shape[1]
    modes = pairs * MZ
    paired = owners in (2, 4, 8)
    order, back_order, last_order = (
        [step for step in steps if step < owners] if paired else [0] for steps in (ORDER, BACK_ORDER, LAST_ORDER)
    )
    blocks = owners if paired else 1
    owner = lax.axis_index("dp").astype(jnp.int32)
    place = jnp.stack([lax.axis_index("space").astype(jnp.int32), owner if paired else jnp.int32(0)])

    plain_table = jnp.asarray(yz_tables(groups, False))
    scaled_table = jnp.asarray(yz_tables(groups, True))
    x_forward, x_inverse = x_tables(groups)
    x_brief = jnp.asarray(x_forward[:, :, : 2 * width * CBLOCK])
    x_forward, x_inverse = jnp.asarray(x_forward), jnp.asarray(x_inverse)

    def mine(array):
        return pl.BlockSpec((None,) + array.shape[1:], lambda i, s: (s[0], 0, 0))

    def others(array):
        return pl.BlockSpec((None,) + array.shape[1:], lambda i, s: (1 - s[0], 0, 0))

    def entire(shape):
        return pl.BlockSpec(shape, lambda i, s: (0,) * len(shape))

    sample = pl.BlockSpec((None, width, channels, cells), lambda i, s: (0, 0, 0, 0))
    spectrum_shape = (MX, count, lanes)
    spectrum = jax.ShapeDtypeStruct(spectrum_shape, f32)
    field_shape = (width, channels, cells)
    u_scratch = [pltpu.VMEM((2 * HALF, channels, cells), bf16)] * 2
    t_scratch = [pltpu.VMEM((HALF * lanes, 2 * groups * count), bf16)] * 2
    params = pltpu.CompilerParams(vmem_limit_bytes=20 * 1024 * 1024)

    def other_core(value):
        return lax.ppermute(value, "space", [(0, 1), (1, 0)])

    spectrum_scratch = [pltpu.VMEM(spectrum_shape, f32)] * 2
    part_shape = (blocks, MX // blocks, count, lanes)
    block_specs = [entire(part_shape[1:])] * (2 * blocks)
    part_type = jax.ShapeDtypeStruct(part_shape, f32)
    table_scratch = pltpu.VMEM(plain_table.shape[1:], bf16)
    own, sent = pl.pallas_call(
        functools.partial(first_kernel, order),
        out_shape=[part_type] * 2,
        in_specs=[pl.BlockSpec(memory_space=pltpu.HBM)] * 3,
        scratch_shapes=[
            pltpu.VMEM((channels // CBLOCK, width, CBLOCK, cells), bf16),
            pltpu.VMEM(x_brief.shape[1:], bf16),
            table_scratch,
            table_scratch,
            pltpu.SemaphoreType.DMA((channels // CBLOCK + 3,)),
        ]
        + u_scratch
        + spectrum_scratch,
        compiler_params=pltpu.CompilerParams(vmem_limit_bytes=62 * 1024 * 1024),
        name="first",
    )(inputs, x_brief, plain_table)

    weight_shape = (modes, channels, lanes)
    weight, own = lax.optimization_barrier((spectral_weight.reshape(weight_shape), own))

    def travel(value, step):
        return lax.ppermute(value, "dp", [(i, i ^ step) for i in range(owners)]) if step else value

    def to_owners(own, sent):
        got = other_core(sent)
        if not paired:
            return [lax.all_to_all((own + got).reshape(owners, modes, lanes), "dp", 0, 0, tiled=True)]
        return [travel((own[i] + got[i]).reshape(1, modes, lanes), step) for i, step in enumerate(order)]

    def from_owners(values, steps, tie=None):
        if not paired:
            values = [lax.all_to_all(values[0], "dp", 0, 0, tiled=True)]
        else:
            values = [travel(values[order.index(step)], step) for step in steps]
        if tie is not None:
            values, tie = lax.optimization_barrier((values, tie))
        values = [value.reshape(part_shape[1:]) for value in values]
        return values + [other_core(value) for value in values], tie

    mode_params = pltpu.CompilerParams(vmem_limit_bytes=14 * 1024 * 1024)

    def estimate(microseconds):
        return pl.CostEstimate(flops=microseconds * 10**9, bytes_accessed=10**5, transcendentals=0)

    def mixing(chunk, values, weights, name):
        return pl.pallas_call(
            functools.partial(mode_kernel, chunk, len(values)),
            out_shape=[jax.ShapeDtypeStruct(value.shape, f32) for value in values],
            scratch_shapes=[pltpu.VMEM((owners, modes, lanes), f32)] * 2,
            compiler_params=mode_params,
            cost_estimate=estimate(1),
            name=name,
        )(*values, *weights)

    large = 48 if modes % 48 == 0 else modes
    large_spec = pl.BlockSpec((large, channels, lanes), lambda i: (i, 0, 0))
    def split_weights(weight):
        return pl.pallas_call(
            split_kernel,
            out_shape=[jax.ShapeDtypeStruct(weight_shape, bf16)] * 2,
            grid=(modes // large,),
            in_specs=[large_spec],
            out_specs=[large_spec] * 2,
            compiler_params=mode_params,
            cost_estimate=estimate(6),
            name="split",
        )(weight)

    owned = to_owners(own, sent)
    mixture = list(mixing(mix_chunk, owned, split_weights(weight), "mix"))
    mixed, _ = from_owners(mixture, back_order)

    field = jax.ShapeDtypeStruct(field_shape, bf16)
    own, sent, slope_high, slope_low = pl.pallas_call(
        functools.partial(middle_kernel, back_order, order),
        out_shape=[part_type] * 2 + [field, field],
        grid_spec=pltpu.PrefetchScalarGridSpec(
            num_scalar_prefetch=1,
            grid=(1,),
            in_specs=[
                *block_specs, sample, sample, entire(pointwise_weight.shape),
                mine(x_inverse), mine(x_forward), mine(scaled_table), others(scaled_table),
            ],
            out_specs=[entire(part_shape)] * 2 + [entire(field_shape)] * 2,
            scratch_shapes=u_scratch + t_scratch + spectrum_scratch + [pltpu.VMEM(field_shape, f32)],
        ),
        compiler_params=params,
        name="middle",
    )(place, *mixed, inputs, cotangent, pointwise_weight, x_inverse, x_forward, scaled_table, scaled_table)
    again, own = lax.optimization_barrier((weight, own))
    slopes = to_owners(own, sent)
    local, *weights = pl.pallas_call(
        local_split_kernel,
        out_shape=[jax.ShapeDtypeStruct(field_shape, f32)] + [jax.ShapeDtypeStruct(weight_shape, bf16)] * 2,
        cost_estimate=estimate(6),
        compiler_params=mode_params,
        name="local",
    )(slope_high, slope_low, pointwise_weight, again)
    turned = mixing(adjoint_chunk, slopes, weights, "adjoint")

    block = 24 if modes % 24 == 0 else modes
    whole = jax.ShapeDtypeStruct(weight_shape, f32)
    weight_spec = pl.BlockSpec((block, channels, lanes), lambda i: (i, 0, 0))
    value_specs = [pl.BlockSpec(value.shape, lambda i: (0, 0, 0)) for value in owned]
    new_weight, new_first, new_second = pl.pallas_call(
        functools.partial(adam_kernel, len(owned)),
        out_shape=[whole] * 3,
        grid=(modes // block,),
        in_specs=value_specs * 2 + [weight_spec] * 3,
        out_specs=[weight_spec] * 3,
        scratch_shapes=[pltpu.VMEM((owners, block, lanes), f32)] * 2,
        compiler_params=pltpu.CompilerParams(vmem_limit_bytes=30 * 1024 * 1024),
        cost_estimate=pl.CostEstimate(flops=10**10, bytes_accessed=3 * 10**7, transcendentals=10**6),
        name="adam",
    )(*owned, *slopes, weight, first_moment.reshape(weight_shape), second_moment.reshape(weight_shape))
    mixed, new_first = from_owners(turned, last_order, new_first)

    out_field = pl.pallas_call(
        functools.partial(last_kernel, last_order),
        out_shape=jax.ShapeDtypeStruct(inputs.shape, bf16),
        grid_spec=pltpu.PrefetchScalarGridSpec(
            num_scalar_prefetch=1,
            grid=(1,),
            in_specs=[*block_specs, entire(field_shape), mine(x_inverse), mine(plain_table), others(plain_table)],
            out_specs=sample,
            scratch_shapes=u_scratch + t_scratch + spectrum_scratch,
        ),
        compiler_params=params,
        name="last",
    )(place, *mixed, local, x_inverse, plain_table, plain_table)
    shape = spectral_weight.shape
    return (out_field, new_weight.reshape(shape), new_first.reshape(shape), new_second.reshape(shape))


def solution(mesh):
    return jax.shard_map(
        body,
        mesh=mesh,
        in_specs=(
            P(("grp", "dp"), "space", None, None),
            P(("grp", "dp"), "space", None, None),
            P(("grp", "space"), "dp", None, None, None),
            P(("grp", "space"), "dp", None, None, None),
            P(("grp", "space"), "dp", None, None, None),
            P("grp", None),
        ),
        out_specs=(
            P(("grp", "dp"), "space", None, None),
            P(("grp", "space"), "dp", None, None, None),
            P(("grp", "space"), "dp", None, None, None),
            P(("grp", "space"), "dp", None, None, None),
        ),
        check_vma=False,
    )
```

```python
import functools
import math

import jax
import jax.numpy as jnp
import ml_dtypes
import numpy as np
from jax import lax
from jax.experimental import pallas as pl
from jax.experimental.pallas import tpu as pltpu
from jax.sharding import PartitionSpec as P

MX = 16
MY = 16
MZ = 9
GX = 32
GY = 16
GZ = 32
HALF = MX // 2 + 1
CBLOCK = 16
ORDER = (0, 1, 2, 3, 4, 5, 6, 7)
BACK_ORDER = (4, 5, 6, 7, 3, 2, 1, 0)
LAST_ORDER = (1, 2, 4, 5, 6, 7, 3, 0)

beta_first = 0.9
beta_second = 0.999
learn_rate = 0.001
adam_epsilon = 1e-08
first_correct = 1.0 - math.exp(1000.0 * math.log(0.9))
second_correct = 1.0 - math.exp(1000.0 * math.log(0.999))

f32 = jnp.float32
bf16 = jnp.bfloat16


def split_np(table):
    high = table.astype(np.float32).astype(ml_dtypes.bfloat16)
    low = (table - high.astype(np.float64)).astype(np.float32).astype(ml_dtypes.bfloat16)
    return high, low


def parity_rows(per_group):
    half = per_group // 2 * MZ
    return [(slot % 2) * half + slot // 2 * MZ + kz for slot in range(per_group) for kz in range(MZ)]


def padded_rows(per_group):
    return -(-(per_group // 2 * MZ) // 8) * 8


def yz_tables(groups, scaled):
    per_group = MY // groups
    y_frequency = np.concatenate([np.arange(MY // 2), np.arange(GY - MY // 2, GY)]).reshape(groups, per_group // 2, 2)
    y_frequency = np.swapaxes(y_frequency, 1, 2)
    y_place = np.repeat(np.arange(GY // 2), GZ)
    z_place = np.tile(np.arange(GZ), GY // 2)
    turns = y_frequency[..., None, None] * y_place / GY + np.arange(MZ)[None, None, None, :, None] * z_place / GZ
    angle = 2.0 * np.pi * (turns % 1.0)
    table = np.stack([np.cos(angle), -np.sin(angle)], axis=2)
    if scaled:
        table = table * (np.where(np.arange(MZ) == 0, 1.0, 2.0) / (GX * GY * GZ))[:, None]
    table = table.reshape(groups, 2, 2, per_group // 2 * MZ, GY // 2 * GZ)
    rows = padded_rows(per_group)
    padded = np.zeros(table.shape[:3] + (rows, table.shape[-1]))
    padded[:, 0, :, : table.shape[3]] = table[:, 0]
    padded[:, 1, :, rows - table.shape[3] :] = table[:, 1]
    padded = padded.reshape(groups, 2, 2 * rows, table.shape[-1])
    return np.concatenate(split_np(padded), axis=2).reshape(groups, 8 * rows, table.shape[-1])


def x_tables(groups):
    width = GX // groups
    place = np.arange(GX).reshape(groups, 1, width)
    angle = 2.0 * np.pi * (np.arange(HALF)[None, :, None] * place % GX) / GX
    table = np.stack([np.cos(angle), -np.sin(angle)], axis=2).reshape(groups, 2 * HALF, width)
    wide = np.einsum("gkx,cd->gkcxd", table, np.eye(CBLOCK)).reshape(groups, 2 * HALF * CBLOCK, width * CBLOCK)
    high, low = split_np(wide)
    forward = np.concatenate([high, low, high], axis=2)
    flip = lambda t: np.swapaxes(t, 1, 2)
    inverse = np.concatenate([flip(high), flip(low), flip(high)], axis=2)
    return forward, np.ascontiguousarray(inverse)


def dot(a, b):
    return lax.dot_general(a, b, (((1,), (0,)), ((), ())), preferred_element_type=f32)


def dot_nt(a, b):
    return lax.dot_general(a, b, (((1,), (1,)), ((), ())), preferred_element_type=f32)


def dot_tn(a, b):
    return lax.dot_general(a, b, (((0,), (0,)), ((), ())), preferred_element_type=f32)


def split(value):
    high = value.astype(bf16)
    return high, (value - high.astype(f32)).astype(bf16)


def lane_sign(shape, first):
    lane = lax.broadcasted_iota(jnp.int32, shape, len(shape) - 1)
    return jnp.where(lane < shape[-1] // 2, first, -first).astype(f32)


def swap(value):
    return pltpu.roll(value, value.shape[-1] // 2, value.ndim - 1)


def to_spectra(channels, fields, x_table, own, other, own_out, other_out, u_high, u_low, ready=None):
    for block in range(channels // CBLOCK):
        pieces = fields(block)
        cells = pieces[0].shape[0]
        stacked = pieces[0] if len(pieces) == 1 else jnp.concatenate(pieces, axis=0)
        result = dot(x_table[:, : cells * len(pieces)], stacked)
        middle = result.shape[-1] // 2
        lower, upper = result[:, :middle], result[:, middle:]
        high, low = split(jnp.concatenate([lower + upper, lower - upper], axis=1))
        rows = pl.ds(block * CBLOCK, CBLOCK)
        shape = (2 * HALF, CBLOCK, high.shape[-1])
        u_high[:, rows, :] = high.reshape(shape)
        u_low[:, rows, :] = low.reshape(shape)
    if ready is not None:
        ready()
    rows = own.shape[0] // 8
    part = 2 * rows
    count = own_out.shape[1]
    overlap = 2 * rows - count
    shared = pl.ds(count - rows, overlap)
    tables = [
        jnp.concatenate([own[2 * part * odd : 2 * part * (odd + 1), :], other[2 * part * odd : 2 * part * (odd + 1), :]], axis=0)
        for odd in range(2)
    ]
    briefs = [
        jnp.concatenate([own[2 * part * odd : 2 * part * odd + part, :], other[2 * part * odd : 2 * part * odd + part, :]], axis=0)
        for odd in range(2)
    ]
    width = 2 * channels
    sign = lane_sign((rows, width), -1.0)
    half_cells = u_high.shape[-1] // 2
    for first in range(0, HALF, 2):
        several = min(2, HALF - first)
        at = pl.ds(2 * first, 2 * several)
        high = u_high[at].reshape(several * width, 2 * half_cells)
        low = u_low[at].reshape(several * width, 2 * half_cells)
        wide = [dot_nt(tables[odd], high[:, half_cells * odd : half_cells * (odd + 1)]) for odd in range(2)]
        small = [dot_nt(briefs[odd], low[:, half_cells * odd : half_cells * (odd + 1)]) for odd in range(2)]
        for which, out in enumerate((own_out, other_out)):
            base = 2 * part * which
            totals = [
                (wide[odd][base : base + part] + wide[odd][base + part : base + 2 * part])
                + small[odd][part * which : part * (which + 1)]
                for odd in range(2)
            ]

            def put(kx, even, odd):
                out[kx, : count - rows] = even[: count - rows]
                out[kx, shared] = even[count - rows :] + odd[:overlap]
                out[kx, rows:] = odd[overlap:]

            for step in range(several):
                kx = first + step
                lanes = slice(step * width, (step + 1) * width)
                real = [total[:rows, lanes] for total in totals]
                imag = [swap(total[rows:, lanes]) for total in totals]
                if kx < MX // 2:
                    put(kx, *[r + i * sign for r, i in zip(real, imag)])
                if kx > 0:
                    put(MX - kx, *[i - r * sign for r, i in zip(real, imag)])


def gather(place, order, sources, target):
    for step, source in zip(order, sources):
        block = source.shape[0]
        target[pl.ds((place[1] ^ step) * block, block)] = source[...]


def scatter(place, order, source, target):
    block = target.shape[1]
    for index, step in enumerate(order):
        target[index] = source[pl.ds((place[1] ^ step) * block, block)]


def from_spectra(channels, own_in, other_in, x_table, own, other, u_high, u_low, t_high, t_low):
    rows = own.shape[0] // 8
    part = 2 * rows
    count = own_in.shape[1]
    width = 2 * channels
    half_cells = own.shape[1]
    sign = lane_sign((count, width), -1.0)
    for kx in range(HALF):
        pieces = []
        for source in (own_in, other_in):
            if kx == 0:
                ahead = source[0]
                real, imag = ahead, ahead * sign
            elif kx == MX // 2:
                behind = source[MX - kx]
                real, imag = -behind * sign, behind
            else:
                ahead, behind = source[kx], source[MX - kx]
                real, imag = ahead - behind * sign, ahead * sign + behind
            pieces += [real, swap(imag)]
        at = pl.ds(kx * width, width)
        for odd, first in enumerate((0, count - rows)):
            turned = jnp.concatenate([piece[first : first + rows] for piece in pieces], axis=0).T
            high, low = split(turned)
            lanes = pl.ds(half_cells * odd, 2 * part)
            t_high[at, lanes] = high
            t_low[at, lanes] = low
    tables = []
    for odd in range(2):
        base = 2 * part * odd
        tables.append(
            [
                jnp.concatenate([own[base + shift : base + shift + part, :], other[base + shift : base + shift + part, :]], axis=0)
                for shift in (0, part)
            ]
        )
    several = 3 if HALF % 3 == 0 else 1
    for first in range(0, HALF, several):
        at = pl.ds(first * width, several * width)
        values = []
        for odd, (table_high, table_low) in enumerate(tables):
            lanes = pl.ds(half_cells * odd, 2 * part)
            high, low = t_high[at, lanes], t_low[at, lanes]
            values.append(dot(high, table_high) + dot(low, table_high) + dot(high, table_low))
        even, odd = values
        value_high, value_low = split(jnp.concatenate([even + odd, even - odd], axis=1))
        shape = (2 * several, channels, 2 * half_cells)
        u_high[pl.ds(2 * first, 2 * several)] = value_high.reshape(shape)
        u_low[pl.ds(2 * first, 2 * several)] = value_low.reshape(shape)

    def block(index):
        rows = pl.ds(index * CBLOCK, CBLOCK)
        shape = (2 * HALF * CBLOCK, u_high.shape[-1])
        high = u_high[:, rows, :].reshape(shape)
        low = u_low[:, rows, :].reshape(shape)
        return dot(x_table[...], jnp.concatenate([high, high, low], axis=0))

    return block


def first_kernel(
    order, field_in, x_in, table_in, own_part, other_part, field, x_table, own, other, sems, u_high, u_low, own_out, other_out
):
    blocks, width, _, cells = field.shape
    space = lax.axis_index("space")
    place = (space, lax.axis_index("dp") if len(order) > 1 else 0)
    copies = [pltpu.make_async_copy(x_in.at[space], x_table, sems.at[0])]
    for block in range(blocks):
        piece = field_in.at[0, :, pl.ds(block * CBLOCK, CBLOCK), :]
        copies.append(pltpu.make_async_copy(piece, field.at[block], sems.at[1 + block]))
    copies.append(pltpu.make_async_copy(table_in.at[space], own, sems.at[1 + blocks]))
    copies.append(pltpu.make_async_copy(table_in.at[1 - space], other, sems.at[2 + blocks]))
    for copy in copies:
        copy.start()
    copies[0].wait()

    def fields(block):
        copies[1 + block].wait()
        piece = field[block].reshape(width * CBLOCK, cells)
        return [piece, piece]

    def ready():
        copies[1 + blocks].wait()
        copies[2 + blocks].wait()

    channels = blocks * CBLOCK
    to_spectra(channels, fields, x_table, own, other, own_out, other_out, u_high, u_low, ready)
    scatter(place, order, other_out, other_part)
    scatter(place, order, own_out, own_part)


def middle_kernel(back_order, order, place, *refs):
    number = len(back_order)
    own_blocks, other_blocks = refs[:number], refs[number : 2 * number]
    field, cotangent, pointwise, x_inverse, x_forward, own, other, *refs = refs[2 * number :]
    own_part, other_part, slope_high, slope_low, u_high, u_low, t_high, t_low, own_in, other_in, pre = refs
    gather(place, back_order, own_blocks, own_in)
    gather(place, back_order, other_blocks, other_in)
    width, channels, cells = field.shape
    block = from_spectra(channels, own_in, other_in, x_inverse, own, other, u_high, u_low, t_high, t_low)
    for index in range(channels // CBLOCK):
        pre[:, pl.ds(index * CBLOCK, CBLOCK), :] = block(index).reshape(width, CBLOCK, cells)
    root = math.sqrt(2.0 / math.pi)
    mixer = jnp.concatenate(split(pointwise[...].T), axis=0)

    @pl.loop(0, width, unroll=4)
    def _(x):
        local = dot(mixer, field[x])
        value = pre[x] + (local[:channels] + local[channels:])
        square = value * value
        tanh = jnp.tanh(root * value * (1.0 + 0.044715 * square))
        slope = 0.5 * (1.0 + tanh) + (0.5 * root) * value * (1.0 - tanh * tanh) * (1.0 + 3.0 * 0.044715 * square)
        slope = slope * cotangent[x].astype(f32)
        high, low = split(slope)
        slope_high[x] = high
        slope_low[x] = low

    def fields(index):
        rows = pl.ds(index * CBLOCK, CBLOCK)
        shape = (width * CBLOCK, cells)
        high = slope_high[:, rows, :].reshape(shape)
        return [high, high, slope_low[:, rows, :].reshape(shape)]

    to_spectra(channels, fields, x_forward, own, other, own_in, other_in, u_high, u_low)
    scatter(place, order, other_in, other_part)
    scatter(place, order, own_in, own_part)


def last_kernel(order, place, *refs):
    number = len(order)
    own_blocks, other_blocks = refs[:number], refs[number : 2 * number]
    local, x_inverse, own, other, out, u_high, u_low, t_high, t_low, own_in, other_in = refs[2 * number :]
    gather(place, order, own_blocks, own_in)
    gather(place, order, other_blocks, other_in)
    width, channels, cells = out.shape
    block = from_spectra(channels, own_in, other_in, x_inverse, own, other, u_high, u_low, t_high, t_low)
    for index in range(channels // CBLOCK):
        rows = pl.ds(index * CBLOCK, CBLOCK)
        value = block(index).reshape(width, CBLOCK, cells) + local[:, rows, :]
        out[:, rows, :] = value.astype(bf16)


def local_gradient(high_in, low_in, pointwise, out):
    channels = pointwise.shape[0]
    high, low = split(pointwise[...])
    both = jnp.concatenate([high, low], axis=0)

    @pl.loop(0, out.shape[0], unroll=4)
    def _(x):
        wide = dot(both, high_in[x])
        out[x] = (wide[:channels] + wide[channels:]) + dot(high, low_in[x])


def pairs_of(count):
    return [list(range(first, min(first + 2, count))) for first in range(0, count, 2)]


def spread_rows(rows, lower):
    if len(rows) == 1:
        half = rows[0].shape[-1] // 2
        return jnp.concatenate([rows[0][:, :half], rows[0][:, half:]], axis=0)
    zero = jnp.zeros_like(rows[0])
    one, two = rows
    return jnp.concatenate(
        [
            jnp.where(lower, one, zero),
            jnp.where(lower, swap(one), zero),
            jnp.where(lower, zero, swap(two)),
            jnp.where(lower, zero, two),
        ],
        axis=0,
    )


def lower_half(shape):
    return lax.broadcasted_iota(jnp.int32, shape, 1) < shape[1] // 2


def mode_chunk(modes):
    return 72 if modes % 72 == 0 else modes


def mode_rows(chunk):
    return parity_rows(chunk // MZ) if chunk > MZ else list(range(chunk))


def stack(refs, target):
    base = 0
    for ref in refs:
        target[pl.ds(base, ref.shape[0])] = ref[...]
        base += ref.shape[0]


def unstack(source, refs):
    base = 0
    for ref in refs:
        ref[...] = source[pl.ds(base, ref.shape[0])]
        base += ref.shape[0]


def split_kernel(weight, high, low):
    high[...], low[...] = split(weight[...])


def local_split_kernel(slope_high, slope_low, pointwise, weight, local, high, low):
    local_gradient(slope_high, slope_low, pointwise, local)
    modes = weight.shape[0]
    chunk = mode_chunk(modes)

    @pl.loop(0, modes // chunk)
    def _(index):
        at = pl.ds(index * chunk, chunk)
        high[at], low[at] = split(weight[at])


def hold_kernel(field, cotangent, x_inverse, x_forward, table, *targets):
    space = lax.axis_index("space")
    values = [field[0], cotangent[0], x_inverse[space], x_forward[space], table[space], table[1 - space]]
    for target, value in zip(targets, values):
        target[...] = value


def mode_kernel(one_chunk, number, *refs):
    sources, weights, refs = refs[:number], refs[number : number + 2], refs[number + 2 :]
    spectra, out = refs[-2:]
    stack(sources, spectra)
    modes = spectra.shape[1]
    chunk = mode_chunk(modes)

    @pl.loop(0, modes // chunk)
    def _(index):
        start = index * chunk
        places = mode_rows(chunk)
        rows = [spectra[:, start + place, :] for place in places]

        def weight(first, count):
            values = [part[pl.ds(start + first, count)] for part in weights]
            return [value.reshape(-1, value.shape[-1]) for value in values]

        for place, value in zip(places, one_chunk(rows, weight)):
            out[:, start + place, :] = value

    unstack(out, refs[:number])


def mix_chunk(rows_of, weight):
    samples, width = rows_of[0].shape
    lower = lower_half((samples, width))
    sign = lane_sign((samples, width), -1.0)
    results = []
    for group in pairs_of(len(rows_of)):
        rows = spread_rows([rows_of[mode] for mode in group], lower)
        high, low = split(rows)
        block_high, block_low = weight(group[0], len(group))
        wide = dot(jnp.concatenate([high, low], axis=0), block_high)
        total = wide[: rows.shape[0]] + wide[rows.shape[0] :] + dot(high, block_low)
        for step, mode in enumerate(group):
            base = 2 * samples * step
            real, imag = total[base : base + samples], total[base + samples : base + 2 * samples]
            results.append(real + swap(imag) * sign)
    return results


def adjoint_chunk(rows_of, weight):
    samples, width = rows_of[0].shape
    lower = lower_half((samples, width))
    sign = lane_sign((samples, width), 1.0)
    results = []
    for group in pairs_of(len(rows_of)):
        rows = []
        for mode in group:
            rows += [rows_of[mode], swap(rows_of[mode]) * sign]
        rows = jnp.concatenate(rows, axis=0)
        high, low = split(rows)
        block_high, block_low = weight(group[0], len(group))
        wide = dot_nt(jnp.concatenate([high, low], axis=0), block_high)
        total = wide[: rows.shape[0]] + wide[rows.shape[0] :] + dot_nt(high, block_low)
        for step in range(len(group)):
            base = 2 * samples * step
            real, imag = total[base : base + samples], total[base + samples : base + 2 * samples]
            if len(group) == 1:
                results.append(jnp.concatenate([real, imag], axis=1))
            elif step == 0:
                results.append(jnp.where(lower, real, swap(imag)))
            else:
                results.append(jnp.where(lower, swap(real), imag))
    return results


def adam_kernel(number, *refs):
    spectra_parts, slope_parts, refs = refs[:number], refs[number : 2 * number], refs[2 * number :]
    weight, first, second, weight_out, first_out, second_out, spectra, slopes, all_spectra, all_slopes = refs
    samples, modes, width = spectra.shape
    start = pl.program_id(0) * modes

    @pl.when(pl.program_id(0) == 0)
    def _():
        places = mode_rows(mode_chunk(all_spectra.shape[1]))
        for parts, target in ((spectra_parts, all_spectra), (slope_parts, all_slopes)):
            base = 0
            for part in parts:
                for first in range(0, part.shape[1], MZ):
                    block = first // len(places) * len(places)
                    source = pl.ds(block + places[first - block], MZ)
                    target[pl.ds(base, part.shape[0]), pl.ds(first, MZ), :] = part[:, source, :]
                base += part.shape[0]

    here = pl.ds(pl.multiple_of(start, 8) if modes % 8 == 0 else 0, modes)
    spectra[...] = all_spectra[:, here, :]
    slopes[...] = all_slopes[:, here, :]
    lower = lower_half((samples, width))
    sign = lane_sign((samples, width), 1.0)
    for group in pairs_of(modes):
        left = spread_rows([spectra[:, mode, :] for mode in group], lower)
        right = []
        for mode in group:
            row = slopes[:, mode, :]
            right += [row, swap(row) * sign]
        right = jnp.concatenate(right, axis=0)
        left_high, left_low = split(left)
        right_high, right_low = split(right)
        gradient = dot_tn(
            jnp.concatenate([left_high, left_low, left_high], axis=0),
            jnp.concatenate([right_high, right_high, right_low], axis=0),
        )
        at = pl.ds(group[0], len(group))
        shape = (len(group),) + weight.shape[1:]
        gradient = gradient.reshape(shape)
        new_first = beta_first * first[at] + (1.0 - beta_first) * gradient
        new_second = beta_second * second[at] + (1.0 - beta_second) * gradient * gradient
        bottom = jnp.sqrt(new_second * (1.0 / second_correct)) + adam_epsilon
        first_out[at] = new_first
        second_out[at] = new_second
        weight_out[at] = weight[at] - (learn_rate / first_correct) * new_first / bottom


def body(inputs, cotangent, spectral_weight, first_moment, second_moment, pointwise_weight):
    groups = lax.axis_size("space")
    owners = lax.axis_size("dp")
    assert groups == 2 and inputs.shape[0] == 1
    per_group = MY // groups
    _, width, channels, cells = inputs.shape
    lanes = 2 * channels
    count = per_group * MZ
    pairs = spectral_weight.shape[1]
    modes = pairs * MZ
    paired = owners in (2, 4, 8)
    order, back_order, last_order = (
        [step for step in steps if step < owners] if paired else [0] for steps in (ORDER, BACK_ORDER, LAST_ORDER)
    )
    blocks = owners if paired else 1
    owner = lax.axis_index("dp").astype(jnp.int32)
    place = jnp.stack([lax.axis_index("space").astype(jnp.int32), owner if paired else jnp.int32(0)])

    plain_table = jnp.asarray(yz_tables(groups, False))
    scaled_table = jnp.asarray(yz_tables(groups, True))
    x_forward, x_inverse = x_tables(groups)
    x_brief = jnp.asarray(x_forward[:, :, : 2 * width * CBLOCK])
    x_forward, x_inverse = jnp.asarray(x_forward), jnp.asarray(x_inverse)

    def mine(array):
        return pl.BlockSpec((None,) + array.shape[1:], lambda i, s: (s[0], 0, 0))

    def others(array):
        return pl.BlockSpec((None,) + array.shape[1:], lambda i, s: (1 - s[0], 0, 0))

    def entire(shape):
        return pl.BlockSpec(shape, lambda i, s: (0,) * len(shape))

    sample = pl.BlockSpec((None, width, channels, cells), lambda i, s: (0, 0, 0, 0))
    spectrum_shape = (MX, count, lanes)
    spectrum = jax.ShapeDtypeStruct(spectrum_shape, f32)
    field_shape = (width, channels, cells)
    u_scratch = [pltpu.VMEM((2 * HALF, channels, cells), bf16)] * 2
    t_scratch = [pltpu.VMEM((HALF * lanes, cells), bf16)] * 2
    params = pltpu.CompilerParams(vmem_limit_bytes=20 * 1024 * 1024)

    def other_core(value):
        return lax.ppermute(value, "space", [(0, 1), (1, 0)])

    spectrum_scratch = [pltpu.VMEM(spectrum_shape, f32)] * 2
    part_shape = (blocks, MX // blocks, count, lanes)
    block_specs = [entire(part_shape[1:])] * (2 * blocks)
    part_type = jax.ShapeDtypeStruct(part_shape, f32)
    table_scratch = pltpu.VMEM(plain_table.shape[1:], bf16)
    own, sent = pl.pallas_call(
        functools.partial(first_kernel, order),
        out_shape=[part_type] * 2,
        in_specs=[pl.BlockSpec(memory_space=pltpu.HBM)] * 3,
        scratch_shapes=[
            pltpu.VMEM((channels // CBLOCK, width, CBLOCK, cells), bf16),
            pltpu.VMEM(x_brief.shape[1:], bf16),
            table_scratch,
            table_scratch,
            pltpu.SemaphoreType.DMA((channels // CBLOCK + 3,)),
        ]
        + u_scratch
        + spectrum_scratch,
        compiler_params=pltpu.CompilerParams(vmem_limit_bytes=62 * 1024 * 1024),
        name="first",
    )(inputs, x_brief, plain_table)

    weight_shape = (modes, channels, lanes)
    weight, own = lax.optimization_barrier((spectral_weight.reshape(weight_shape), own))

    def travel(value, step):
        return lax.ppermute(value, "dp", [(i, i ^ step) for i in range(owners)]) if step else value

    def to_owners(own, sent):
        got = other_core(sent)
        if not paired:
            total = own + got
            places = parity_rows(per_group)[::MZ]
            total = jnp.concatenate([total[:, :, place : place + MZ] for place in places], axis=2)
            return [lax.all_to_all(total.reshape(owners, modes, lanes), "dp", 0, 0, tiled=True)]
        return [travel((own[i] + got[i]).reshape(1, modes, lanes), step) for i, step in enumerate(order)]

    def from_owners(values, steps, tie=None):
        if not paired:
            value = lax.all_to_all(values[0], "dp", 0, 0, tiled=True).reshape(part_shape)
            slots = list(range(0, per_group, 2)) + list(range(1, per_group, 2))
            values = [jnp.concatenate([value[:, :, slot * MZ : (slot + 1) * MZ] for slot in slots], axis=2)]
        else:
            values = [travel(values[order.index(step)], step) for step in steps]
        if tie is not None:
            values, tie = lax.optimization_barrier((values, tie))
        values = [value.reshape(part_shape[1:]) for value in values]
        return values + [other_core(value) for value in values], tie

    mode_params = pltpu.CompilerParams(vmem_limit_bytes=14 * 1024 * 1024)

    def estimate(microseconds):
        return pl.CostEstimate(flops=microseconds * 10**9, bytes_accessed=10**5, transcendentals=0)

    def mixing(chunk, values, weights, name):
        return pl.pallas_call(
            functools.partial(mode_kernel, chunk, len(values)),
            out_shape=[jax.ShapeDtypeStruct(value.shape, f32) for value in values],
            scratch_shapes=[pltpu.VMEM((owners, modes, lanes), f32)] * 2,
            compiler_params=mode_params,
            cost_estimate=estimate(1),
            name=name,
        )(*values, *weights)

    large = 48 if modes % 48 == 0 else modes
    large_spec = pl.BlockSpec((large, channels, lanes), lambda i: (i, 0, 0))
    def split_weights(weight):
        return pl.pallas_call(
            split_kernel,
            out_shape=[jax.ShapeDtypeStruct(weight_shape, bf16)] * 2,
            grid=(modes // large,),
            in_specs=[large_spec],
            out_specs=[large_spec] * 2,
            compiler_params=mode_params,
            cost_estimate=estimate(6),
            name="split",
        )(weight)

    owned = to_owners(own, sent)
    mixture = list(mixing(mix_chunk, owned, split_weights(weight), "mix"))
    mixed, _ = from_owners(mixture, back_order)

    field = jax.ShapeDtypeStruct(field_shape, bf16)
    own, sent, slope_high, slope_low = pl.pallas_call(
        functools.partial(middle_kernel, back_order, order),
        out_shape=[part_type] * 2 + [field, field],
        grid_spec=pltpu.PrefetchScalarGridSpec(
            num_scalar_prefetch=1,
            grid=(1,),
            in_specs=[
                *block_specs, sample, sample, entire(pointwise_weight.shape),
                mine(x_inverse), mine(x_forward), mine(scaled_table), others(scaled_table),
            ],
            out_specs=[entire(part_shape)] * 2 + [entire(field_shape)] * 2,
            scratch_shapes=u_scratch + t_scratch + spectrum_scratch + [pltpu.VMEM(field_shape, f32)],
        ),
        compiler_params=params,
        name="middle",
    )(place, *mixed, inputs, cotangent, pointwise_weight, x_inverse, x_forward, scaled_table, scaled_table)
    again, own = lax.optimization_barrier((weight, own))
    slopes = to_owners(own, sent)
    local, *weights = pl.pallas_call(
        local_split_kernel,
        out_shape=[jax.ShapeDtypeStruct(field_shape, f32)] + [jax.ShapeDtypeStruct(weight_shape, bf16)] * 2,
        cost_estimate=estimate(6),
        compiler_params=mode_params,
        name="local",
    )(slope_high, slope_low, pointwise_weight, again)
    turned = mixing(adjoint_chunk, slopes, weights, "adjoint")

    block = 24 if modes % 24 == 0 else modes
    whole = jax.ShapeDtypeStruct(weight_shape, f32)
    weight_spec = pl.BlockSpec((block, channels, lanes), lambda i: (i, 0, 0))
    value_specs = [pl.BlockSpec(value.shape, lambda i: (0, 0, 0)) for value in owned]
    new_weight, new_first, new_second = pl.pallas_call(
        functools.partial(adam_kernel, len(owned)),
        out_shape=[whole] * 3,
        grid=(modes // block,),
        in_specs=value_specs * 2 + [weight_spec] * 3,
        out_specs=[weight_spec] * 3,
        scratch_shapes=[pltpu.VMEM((owners, rows, lanes), f32) for rows in (block, block, modes, modes)],
        compiler_params=pltpu.CompilerParams(vmem_limit_bytes=30 * 1024 * 1024),
        cost_estimate=pl.CostEstimate(flops=10**10, bytes_accessed=3 * 10**7, transcendentals=10**6),
        name="adam",
    )(*owned, *slopes, weight, first_moment.reshape(weight_shape), second_moment.reshape(weight_shape))
    mixed, new_first = from_owners(turned, last_order, new_first)

    out_field = pl.pallas_call(
        functools.partial(last_kernel, last_order),
        out_shape=jax.ShapeDtypeStruct(inputs.shape, bf16),
        grid_spec=pltpu.PrefetchScalarGridSpec(
            num_scalar_prefetch=1,
            grid=(1,),
            in_specs=[*block_specs, entire(field_shape), mine(x_inverse), mine(plain_table), others(plain_table)],
            out_specs=sample,
            scratch_shapes=u_scratch + t_scratch + spectrum_scratch,
        ),
        compiler_params=params,
        name="last",
    )(place, *mixed, local, x_inverse, plain_table, plain_table)
    shape = spectral_weight.shape
    return (out_field, new_weight.reshape(shape), new_first.reshape(shape), new_second.reshape(shape))


def solution(mesh):
    return jax.shard_map(
        body,
        mesh=mesh,
        in_specs=(
            P(("grp", "dp"), "space", None, None),
            P(("grp", "dp"), "space", None, None),
            P(("grp", "space"), "dp", None, None, None),
            P(("grp", "space"), "dp", None, None, None),
            P(("grp", "space"), "dp", None, None, None),
            P("grp", None),
        ),
        out_specs=(
            P(("grp", "dp"), "space", None, None),
            P(("grp", "space"), "dp", None, None, None),
            P(("grp", "space"), "dp", None, None, None),
            P(("grp", "space"), "dp", None, None, None),
        ),
        check_vma=False,
    )
```

```python
import functools
import math

import jax
import jax.numpy as jnp
import ml_dtypes
import numpy as np
from jax import lax
from jax.experimental import pallas as pl
from jax.experimental.pallas import tpu as pltpu
from jax.sharding import PartitionSpec as P

MX = 16
MY = 16
MZ = 9
GX = 32
GY = 16
GZ = 32
HALF = MX // 2 + 1
CBLOCK = 16
ORDER = (0, 1, 2, 3, 4, 5, 6, 7)
BACK_ORDER = (4, 5, 6, 7, 3, 2, 1, 0)
LAST_ORDER = (1, 2, 4, 5, 6, 7, 3, 0)

beta_first = 0.9
beta_second = 0.999
learn_rate = 0.001
adam_epsilon = 1e-08
first_correct = 1.0 - math.exp(1000.0 * math.log(0.9))
second_correct = 1.0 - math.exp(1000.0 * math.log(0.999))

f32 = jnp.float32
bf16 = jnp.bfloat16


def split_np(table):
    high = table.astype(np.float32).astype(ml_dtypes.bfloat16)
    low = (table - high.astype(np.float64)).astype(np.float32).astype(ml_dtypes.bfloat16)
    return high, low


def parity_rows(per_group):
    half = per_group // 2 * MZ
    return [(slot % 2) * half + slot // 2 * MZ + kz for slot in range(per_group) for kz in range(MZ)]


def padded_rows(per_group):
    return -(-(per_group // 2 * MZ) // 8) * 8


def yz_tables(groups, scaled):
    per_group = MY // groups
    y_frequency = np.concatenate([np.arange(MY // 2), np.arange(GY - MY // 2, GY)]).reshape(groups, per_group // 2, 2)
    y_frequency = np.swapaxes(y_frequency, 1, 2)
    y_place = np.repeat(np.arange(GY // 2), GZ)
    z_place = np.tile(np.arange(GZ), GY // 2)
    turns = y_frequency[..., None, None] * y_place / GY + np.arange(MZ)[None, None, None, :, None] * z_place / GZ
    angle = 2.0 * np.pi * (turns % 1.0)
    table = np.stack([np.cos(angle), -np.sin(angle)], axis=2)
    if scaled:
        table = table * (np.where(np.arange(MZ) == 0, 1.0, 2.0) / (GX * GY * GZ))[:, None]
    table = table.reshape(groups, 2, 2, per_group // 2 * MZ, GY // 2 * GZ)
    rows = padded_rows(per_group)
    padded = np.zeros(table.shape[:3] + (rows, table.shape[-1]))
    padded[:, 0, :, : table.shape[3]] = table[:, 0]
    padded[:, 1, :, rows - table.shape[3] :] = table[:, 1]
    padded = padded.reshape(groups, 2, 2 * rows, table.shape[-1])
    return np.concatenate(split_np(padded), axis=2).reshape(groups, 8 * rows, table.shape[-1])


def x_tables(groups):
    width = GX // groups
    place = np.arange(width).reshape(1, 1, width)
    angle = 2.0 * np.pi * (np.arange(HALF)[None, :, None] * place % GX) / GX
    table = np.stack([np.cos(angle), -np.sin(angle)], axis=2).reshape(1, 2 * HALF, width)
    wide = np.einsum("gkx,cd->gkcxd", table, np.eye(CBLOCK)).reshape(1, 2 * HALF * CBLOCK, width * CBLOCK)
    high, low = split_np(wide)
    turned = np.swapaxes(np.concatenate([high, low, high], axis=1), 1, 2)
    return np.concatenate([high, low], axis=2)[0], np.ascontiguousarray(turned[0])


def dot(a, b):
    return lax.dot_general(a, b, (((1,), (0,)), ((), ())), preferred_element_type=f32)


def dot_nt(a, b):
    return lax.dot_general(a, b, (((1,), (1,)), ((), ())), preferred_element_type=f32)


def dot_tn(a, b):
    return lax.dot_general(a, b, (((0,), (0,)), ((), ())), preferred_element_type=f32)


def split(value):
    high = value.astype(bf16)
    return high, (value - high.astype(f32)).astype(bf16)


def lane_sign(shape, first):
    lane = lax.broadcasted_iota(jnp.int32, shape, len(shape) - 1)
    return jnp.where(lane < shape[-1] // 2, first, -first).astype(f32)


def swap(value):
    return pltpu.roll(value, value.shape[-1] // 2, value.ndim - 1)


def turning(space):
    return jnp.where(space == 1, -1.0, 1.0).astype(f32)


def to_spectra(turn, channels, fields, x_table, own, other, own_out, other_out, u_high, u_low, ready=None):
    for block in range(channels // CBLOCK):
        pieces = fields(block)
        cells = pieces[0].shape[0]
        result = dot(x_table[...], jnp.concatenate([pieces[0], pieces[0]], axis=0))
        if len(pieces) > 1:
            result = result + dot(x_table[:, :cells], pieces[1])
        middle = result.shape[-1] // 2
        lower, upper = result[:, :middle], result[:, middle:]
        high, low = split(jnp.concatenate([lower + upper, lower - upper], axis=1))
        rows = pl.ds(block * CBLOCK, CBLOCK)
        shape = (2 * HALF, CBLOCK, high.shape[-1])
        u_high[:, rows, :] = high.reshape(shape)
        u_low[:, rows, :] = low.reshape(shape)
    if ready is not None:
        ready()
    rows = own.shape[0] // 8
    part = 2 * rows
    count = own_out.shape[1]
    overlap = 2 * rows - count
    shared = pl.ds(count - rows, overlap)
    tables = [
        jnp.concatenate([own[2 * part * odd : 2 * part * (odd + 1), :], other[2 * part * odd : 2 * part * (odd + 1), :]], axis=0)
        for odd in range(2)
    ]
    briefs = [
        jnp.concatenate([own[2 * part * odd : 2 * part * odd + part, :], other[2 * part * odd : 2 * part * odd + part, :]], axis=0)
        for odd in range(2)
    ]
    width = 2 * channels
    sign = lane_sign((rows, width), -1.0)
    half_cells = u_high.shape[-1] // 2
    for first in range(0, HALF, 2):
        several = min(2, HALF - first)
        at = pl.ds(2 * first, 2 * several)
        high = u_high[at].reshape(several * width, 2 * half_cells)
        low = u_low[at].reshape(several * width, 2 * half_cells)
        wide = [dot_nt(tables[odd], high[:, half_cells * odd : half_cells * (odd + 1)]) for odd in range(2)]
        small = [dot_nt(briefs[odd], low[:, half_cells * odd : half_cells * (odd + 1)]) for odd in range(2)]
        for which, out in enumerate((own_out, other_out)):
            base = 2 * part * which
            totals = [
                (wide[odd][base : base + part] + wide[odd][base + part : base + 2 * part])
                + small[odd][part * which : part * (which + 1)]
                for odd in range(2)
            ]

            def put(kx, even, odd):
                out[kx, : count - rows] = even[: count - rows]
                out[kx, shared] = even[count - rows :] + odd[:overlap]
                out[kx, rows:] = odd[overlap:]

            for step in range(several):
                kx = first + step
                lanes = slice(step * width, (step + 1) * width)
                parts = [total[:, lanes] * turn if kx % 2 == 1 else total[:, lanes] for total in totals]
                real = [value[:rows] for value in parts]
                imag = [swap(value[rows:]) for value in parts]
                if kx < MX // 2:
                    put(kx, *[r + i * sign for r, i in zip(real, imag)])
                if kx > 0:
                    put(MX - kx, *[i - r * sign for r, i in zip(real, imag)])


def gather(place, order, sources, target):
    for step, source in zip(order, sources):
        block = source.shape[0]
        target[pl.ds((place[1] ^ step) * block, block)] = source[...]


def scatter(place, order, source, target):
    block = target.shape[1]
    for index, step in enumerate(order):
        target[index] = source[pl.ds((place[1] ^ step) * block, block)]


def from_spectra(turn, channels, own_in, other_in, back_to_cells, own, other, u_high, u_low, t_high, t_low):
    rows = own.shape[0] // 8
    part = 2 * rows
    count = own_in.shape[1]
    width = 2 * channels
    half_cells = own.shape[1]
    sign = lane_sign((count, width), -1.0)
    for kx in range(HALF):
        pieces = []
        for source in (own_in, other_in):
            if kx == 0:
                ahead = source[0]
                real, imag = ahead, ahead * sign
            elif kx == MX // 2:
                behind = source[MX - kx]
                real, imag = -behind * sign, behind
            else:
                ahead, behind = source[kx], source[MX - kx]
                real, imag = ahead - behind * sign, ahead * sign + behind
            if kx % 2 == 1:
                real, imag = real * turn, imag * turn
            pieces += [real, swap(imag)]
        at = pl.ds(kx * width, width)
        for odd, first in enumerate((0, count - rows)):
            turned = jnp.concatenate([piece[first : first + rows] for piece in pieces], axis=0).T
            high, low = split(turned)
            lanes = pl.ds(half_cells * odd, 2 * part)
            t_high[at, lanes] = high
            t_low[at, lanes] = low
    tables = []
    for odd in range(2):
        base = 2 * part * odd
        tables.append(
            [
                jnp.concatenate([own[base + shift : base + shift + part, :], other[base + shift : base + shift + part, :]], axis=0)
                for shift in (0, part)
            ]
        )
    several = 3 if HALF % 3 == 0 else 1
    for first in range(0, HALF, several):
        at = pl.ds(first * width, several * width)
        values = []
        for odd, (table_high, table_low) in enumerate(tables):
            lanes = pl.ds(half_cells * odd, 2 * part)
            high, low = t_high[at, lanes], t_low[at, lanes]
            values.append(dot(high, table_high) + dot(low, table_high) + dot(high, table_low))
        even, odd = values
        value_high, value_low = split(jnp.concatenate([even + odd, even - odd], axis=1))
        shape = (2 * several, channels, 2 * half_cells)
        u_high[pl.ds(2 * first, 2 * several)] = value_high.reshape(shape)
        u_low[pl.ds(2 * first, 2 * several)] = value_low.reshape(shape)


    def block(index):
        rows = pl.ds(index * CBLOCK, CBLOCK)
        shape = (2 * HALF * CBLOCK, u_high.shape[-1])
        high = u_high[:, rows, :].reshape(shape)
        low = u_low[:, rows, :].reshape(shape)
        return back_to_cells(high, low)

    return block


def first_kernel(
    order, field_in, x_in, table_in, own_part, other_part, field, x_table, own, other, sems, u_high, u_low, own_out, other_out
):
    blocks, width, _, cells = field.shape
    space = lax.axis_index("space")
    place = (space, lax.axis_index("dp") if len(order) > 1 else 0)
    copies = [pltpu.make_async_copy(x_in, x_table, sems.at[0])]
    for block in range(blocks):
        piece = field_in.at[0, :, pl.ds(block * CBLOCK, CBLOCK), :]
        copies.append(pltpu.make_async_copy(piece, field.at[block], sems.at[1 + block]))
    copies.append(pltpu.make_async_copy(table_in.at[space], own, sems.at[1 + blocks]))
    copies.append(pltpu.make_async_copy(table_in.at[1 - space], other, sems.at[2 + blocks]))
    for copy in copies:
        copy.start()
    copies[0].wait()

    def fields(block):
        copies[1 + block].wait()
        piece = field[block].reshape(width * CBLOCK, cells)
        return [piece]

    def ready():
        copies[1 + blocks].wait()
        copies[2 + blocks].wait()

    channels = blocks * CBLOCK
    to_spectra(turning(space), channels, fields, x_table, own, other, own_out, other_out, u_high, u_low, ready)
    scatter(place, order, other_out, other_part)
    scatter(place, order, own_out, own_part)


def middle_kernel(back_order, order, place, *refs):
    number = len(back_order)
    own_blocks, other_blocks = refs[:number], refs[number : 2 * number]
    field, cotangent, pointwise, x_table, own, other, *refs = refs[2 * number :]
    own_part, other_part, slope_high, slope_low, u_high, u_low, t_high, t_low, own_in, other_in, pre = refs
    gather(place, back_order, own_blocks, own_in)
    gather(place, back_order, other_blocks, other_in)
    width, channels, cells = field.shape
    places = x_table.shape[1] // 2
    turned = x_table[...].astype(f32).T.astype(bf16)

    def product(high, low):
        return (dot(turned[:places], high) + dot(turned[places:], high)) + dot(turned[:places], low)

    block = from_spectra(turning(place[0]), channels, own_in, other_in, product, own, other, u_high, u_low, t_high, t_low)
    for index in range(channels // CBLOCK):
        pre[:, pl.ds(index * CBLOCK, CBLOCK), :] = block(index).reshape(width, CBLOCK, cells)
    root = math.sqrt(2.0 / math.pi)
    mixer = jnp.concatenate(split(pointwise[...].T), axis=0)

    @pl.loop(0, width, unroll=4)
    def _(x):
        local = dot(mixer, field[x])
        value = pre[x] + (local[:channels] + local[channels:])
        square = value * value
        tanh = jnp.tanh(root * value * (1.0 + 0.044715 * square))
        slope = 0.5 * (1.0 + tanh) + (0.5 * root) * value * (1.0 - tanh * tanh) * (1.0 + 3.0 * 0.044715 * square)
        slope = slope * cotangent[x].astype(f32)
        high, low = split(slope)
        slope_high[x] = high
        slope_low[x] = low

    def fields(index):
        rows = pl.ds(index * CBLOCK, CBLOCK)
        shape = (width * CBLOCK, cells)
        high = slope_high[:, rows, :].reshape(shape)
        return [high, slope_low[:, rows, :].reshape(shape)]

    to_spectra(turning(place[0]), channels, fields, x_table, own, other, own_in, other_in, u_high, u_low)
    scatter(place, order, other_in, other_part)
    scatter(place, order, own_in, own_part)


def last_kernel(order, place, *refs):
    number = len(order)
    own_blocks, other_blocks = refs[:number], refs[number : 2 * number]
    local, x_inverse, own, other, out, u_high, u_low, t_high, t_low, own_in, other_in = refs[2 * number :]
    gather(place, order, own_blocks, own_in)
    gather(place, order, other_blocks, other_in)
    width, channels, cells = out.shape
    product = lambda high, low: dot(x_inverse[...], jnp.concatenate([high, high, low], axis=0))
    block = from_spectra(turning(place[0]), channels, own_in, other_in, product, own, other, u_high, u_low, t_high, t_low)
    for index in range(channels // CBLOCK):
        rows = pl.ds(index * CBLOCK, CBLOCK)
        value = block(index).reshape(width, CBLOCK, cells) + local[:, rows, :]
        out[:, rows, :] = value.astype(bf16)


def local_gradient(high_in, low_in, pointwise, out):
    channels = pointwise.shape[0]
    high, low = split(pointwise[...])
    both = jnp.concatenate([high, low], axis=0)

    @pl.loop(0, out.shape[0], unroll=4)
    def _(x):
        wide = dot(both, high_in[x])
        out[x] = (wide[:channels] + wide[channels:]) + dot(high, low_in[x])


def pairs_of(count):
    return [list(range(first, min(first + 2, count))) for first in range(0, count, 2)]


def spread_rows(rows, lower):
    if len(rows) == 1:
        half = rows[0].shape[-1] // 2
        return jnp.concatenate([rows[0][:, :half], rows[0][:, half:]], axis=0)
    zero = jnp.zeros_like(rows[0])
    one, two = rows
    return jnp.concatenate(
        [
            jnp.where(lower, one, zero),
            jnp.where(lower, swap(one), zero),
            jnp.where(lower, zero, swap(two)),
            jnp.where(lower, zero, two),
        ],
        axis=0,
    )


def lower_half(shape):
    return lax.broadcasted_iota(jnp.int32, shape, 1) < shape[1] // 2


def mode_chunk(modes):
    return 72 if modes % 72 == 0 else modes


def mode_rows(chunk):
    return parity_rows(chunk // MZ) if chunk > MZ else list(range(chunk))


def stack(refs, target):
    base = 0
    for ref in refs:
        target[pl.ds(base, ref.shape[0])] = ref[...]
        base += ref.shape[0]


def unstack(source, refs):
    base = 0
    for ref in refs:
        ref[...] = source[pl.ds(base, ref.shape[0])]
        base += ref.shape[0]


def split_kernel(weight, high, low):
    high[...], low[...] = split(weight[...])


def local_split_kernel(slope_high, slope_low, pointwise, weight, local, high, low):
    local_gradient(slope_high, slope_low, pointwise, local)
    modes = weight.shape[0]
    chunk = mode_chunk(modes)

    @pl.loop(0, modes // chunk)
    def _(index):
        at = pl.ds(index * chunk, chunk)
        high[at], low[at] = split(weight[at])


def mode_kernel(one_chunk, number, *refs):
    sources, weights, refs = refs[:number], refs[number : number + 2], refs[number + 2 :]
    spectra, out = refs[-2:]
    stack(sources, spectra)
    modes = spectra.shape[1]
    chunk = mode_chunk(modes)

    @pl.loop(0, modes // chunk)
    def _(index):
        start = index * chunk
        places = mode_rows(chunk)
        rows = [spectra[:, start + place, :] for place in places]

        def weight(first, count):
            values = [part[pl.ds(start + first, count)] for part in weights]
            return [value.reshape(-1, value.shape[-1]) for value in values]

        for place, value in zip(places, one_chunk(rows, weight)):
            out[:, start + place, :] = value

    unstack(out, refs[:number])


def mix_chunk(rows_of, weight):
    samples, width = rows_of[0].shape
    lower = lower_half((samples, width))
    sign = lane_sign((samples, width), -1.0)
    results = []
    for group in pairs_of(len(rows_of)):
        rows = spread_rows([rows_of[mode] for mode in group], lower)
        high, low = split(rows)
        block_high, block_low = weight(group[0], len(group))
        wide = dot(jnp.concatenate([high, low], axis=0), block_high)
        total = wide[: rows.shape[0]] + wide[rows.shape[0] :] + dot(high, block_low)
        for step, mode in enumerate(group):
            base = 2 * samples * step
            real, imag = total[base : base + samples], total[base + samples : base + 2 * samples]
            results.append(real + swap(imag) * sign)
    return results


def adjoint_chunk(rows_of, weight):
    samples, width = rows_of[0].shape
    lower = lower_half((samples, width))
    sign = lane_sign((samples, width), 1.0)
    results = []
    for group in pairs_of(len(rows_of)):
        rows = []
        for mode in group:
            rows += [rows_of[mode], swap(rows_of[mode]) * sign]
        rows = jnp.concatenate(rows, axis=0)
        high, low = split(rows)
        block_high, block_low = weight(group[0], len(group))
        wide = dot_nt(jnp.concatenate([high, low], axis=0), block_high)
        total = wide[: rows.shape[0]] + wide[rows.shape[0] :] + dot_nt(high, block_low)
        for step in range(len(group)):
            base = 2 * samples * step
            real, imag = total[base : base + samples], total[base + samples : base + 2 * samples]
            if len(group) == 1:
                results.append(jnp.concatenate([real, imag], axis=1))
            elif step == 0:
                results.append(jnp.where(lower, real, swap(imag)))
            else:
                results.append(jnp.where(lower, swap(real), imag))
    return results


def adam_kernel(number, *refs):
    spectra_parts, slope_parts, refs = refs[:number], refs[number : 2 * number], refs[2 * number :]
    weight, first, second, weight_out, first_out, second_out, spectra, slopes, all_spectra, all_slopes = refs
    samples, modes, width = spectra.shape
    start = pl.program_id(0) * modes

    @pl.when(pl.program_id(0) == 0)
    def _():
        places = mode_rows(mode_chunk(all_spectra.shape[1]))
        for parts, target in ((spectra_parts, all_spectra), (slope_parts, all_slopes)):
            base = 0
            for part in parts:
                for first in range(0, part.shape[1], MZ):
                    block = first // len(places) * len(places)
                    source = pl.ds(block + places[first - block], MZ)
                    target[pl.ds(base, part.shape[0]), pl.ds(first, MZ), :] = part[:, source, :]
                base += part.shape[0]

    here = pl.ds(pl.multiple_of(start, 8) if modes % 8 == 0 else 0, modes)
    spectra[...] = all_spectra[:, here, :]
    slopes[...] = all_slopes[:, here, :]
    lower = lower_half((samples, width))
    sign = lane_sign((samples, width), 1.0)
    for group in pairs_of(modes):
        left = spread_rows([spectra[:, mode, :] for mode in group], lower)
        right = []
        for mode in group:
            row = slopes[:, mode, :]
            right += [row, swap(row) * sign]
        right = jnp.concatenate(right, axis=0)
        left_high, left_low = split(left)
        right_high, right_low = split(right)
        gradient = dot_tn(
            jnp.concatenate([left_high, left_low, left_high], axis=0),
            jnp.concatenate([right_high, right_high, right_low], axis=0),
        )
        at = pl.ds(group[0], len(group))
        shape = (len(group),) + weight.shape[1:]
        gradient = gradient.reshape(shape)
        new_first = beta_first * first[at] + (1.0 - beta_first) * gradient
        new_second = beta_second * second[at] + (1.0 - beta_second) * gradient * gradient
        bottom = jnp.sqrt(new_second * (1.0 / second_correct)) + adam_epsilon
        first_out[at] = new_first
        second_out[at] = new_second
        weight_out[at] = weight[at] - (learn_rate / first_correct) * new_first / bottom


def body(inputs, cotangent, spectral_weight, first_moment, second_moment, pointwise_weight):
    groups = lax.axis_size("space")
    owners = lax.axis_size("dp")
    assert groups == 2 and inputs.shape[0] == 1
    per_group = MY // groups
    _, width, channels, cells = inputs.shape
    lanes = 2 * channels
    count = per_group * MZ
    pairs = spectral_weight.shape[1]
    modes = pairs * MZ
    paired = owners in (2, 4, 8)
    order, back_order, last_order = (
        [step for step in steps if step < owners] if paired else [0] for steps in (ORDER, BACK_ORDER, LAST_ORDER)
    )
    blocks = owners if paired else 1
    owner = lax.axis_index("dp").astype(jnp.int32)
    place = jnp.stack([lax.axis_index("space").astype(jnp.int32), owner if paired else jnp.int32(0)])

    plain_table = jnp.asarray(yz_tables(groups, False))
    scaled_table = jnp.asarray(yz_tables(groups, True))
    x_table, x_inverse = map(jnp.asarray, x_tables(groups))

    def mine(array):
        return pl.BlockSpec((None,) + array.shape[1:], lambda i, s: (s[0], 0, 0))

    def others(array):
        return pl.BlockSpec((None,) + array.shape[1:], lambda i, s: (1 - s[0], 0, 0))

    def entire(shape):
        return pl.BlockSpec(shape, lambda i, s: (0,) * len(shape))

    sample = pl.BlockSpec((None, width, channels, cells), lambda i, s: (0, 0, 0, 0))
    spectrum_shape = (MX, count, lanes)
    spectrum = jax.ShapeDtypeStruct(spectrum_shape, f32)
    field_shape = (width, channels, cells)
    u_scratch = [pltpu.VMEM((2 * HALF, channels, cells), bf16)] * 2
    t_scratch = [pltpu.VMEM((HALF * lanes, cells), bf16)] * 2
    params = pltpu.CompilerParams(vmem_limit_bytes=20 * 1024 * 1024)

    def other_core(value):
        return lax.ppermute(value, "space", [(0, 1), (1, 0)])

    spectrum_scratch = [pltpu.VMEM(spectrum_shape, f32)] * 2
    part_shape = (blocks, MX // blocks, count, lanes)
    block_specs = [entire(part_shape[1:])] * (2 * blocks)
    part_type = jax.ShapeDtypeStruct(part_shape, f32)
    table_scratch = pltpu.VMEM(plain_table.shape[1:], bf16)
    own, sent = pl.pallas_call(
        functools.partial(first_kernel, order),
        out_shape=[part_type] * 2,
        in_specs=[pl.BlockSpec(memory_space=pltpu.HBM)] * 3,
        scratch_shapes=[
            pltpu.VMEM((channels // CBLOCK, width, CBLOCK, cells), bf16),
            pltpu.VMEM(x_table.shape, bf16),
            table_scratch,
            table_scratch,
            pltpu.SemaphoreType.DMA((channels // CBLOCK + 3,)),
        ]
        + u_scratch
        + spectrum_scratch,
        compiler_params=pltpu.CompilerParams(vmem_limit_bytes=62 * 1024 * 1024),
        name="first",
    )(inputs, x_table, plain_table)

    weight_shape = (modes, channels, lanes)
    weight, own = lax.optimization_barrier((spectral_weight.reshape(weight_shape), own))

    def travel(value, step):
        return lax.ppermute(value, "dp", [(i, i ^ step) for i in range(owners)]) if step else value

    def to_owners(own, sent):
        got = other_core(sent)
        if not paired:
            total = own + got
            places = parity_rows(per_group)[::MZ]
            total = jnp.concatenate([total[:, :, place : place + MZ] for place in places], axis=2)
            return [lax.all_to_all(total.reshape(owners, modes, lanes), "dp", 0, 0, tiled=True)]
        return [travel((own[i] + got[i]).reshape(1, modes, lanes), step) for i, step in enumerate(order)]

    def from_owners(values, steps, tie=None):
        if not paired:
            value = lax.all_to_all(values[0], "dp", 0, 0, tiled=True).reshape(part_shape)
            slots = list(range(0, per_group, 2)) + list(range(1, per_group, 2))
            values = [jnp.concatenate([value[:, :, slot * MZ : (slot + 1) * MZ] for slot in slots], axis=2)]
        else:
            values = [travel(values[order.index(step)], step) for step in steps]
        if tie is not None:
            values, tie = lax.optimization_barrier((values, tie))
        values = [value.reshape(part_shape[1:]) for value in values]
        return values + [other_core(value) for value in values], tie

    mode_params = pltpu.CompilerParams(vmem_limit_bytes=14 * 1024 * 1024)

    def estimate(microseconds):
        return pl.CostEstimate(flops=microseconds * 10**9, bytes_accessed=10**5, transcendentals=0)

    def mixing(chunk, values, weights, name):
        return pl.pallas_call(
            functools.partial(mode_kernel, chunk, len(values)),
            out_shape=[jax.ShapeDtypeStruct(value.shape, f32) for value in values],
            scratch_shapes=[pltpu.VMEM((owners, modes, lanes), f32)] * 2,
            compiler_params=mode_params,
            cost_estimate=estimate(1),
            name=name,
        )(*values, *weights)

    large = 48 if modes % 48 == 0 else modes
    large_spec = pl.BlockSpec((large, channels, lanes), lambda i: (i, 0, 0))
    def split_weights(weight):
        return pl.pallas_call(
            split_kernel,
            out_shape=[jax.ShapeDtypeStruct(weight_shape, bf16)] * 2,
            grid=(modes // large,),
            in_specs=[large_spec],
            out_specs=[large_spec] * 2,
            compiler_params=mode_params,
            cost_estimate=estimate(6),
            name="split",
        )(weight)

    owned = to_owners(own, sent)
    mixture = list(mixing(mix_chunk, owned, split_weights(weight), "mix"))
    mixed, _ = from_owners(mixture, back_order)

    field = jax.ShapeDtypeStruct(field_shape, bf16)
    own, sent, slope_high, slope_low = pl.pallas_call(
        functools.partial(middle_kernel, back_order, order),
        out_shape=[part_type] * 2 + [field, field],
        grid_spec=pltpu.PrefetchScalarGridSpec(
            num_scalar_prefetch=1,
            grid=(1,),
            in_specs=[
                *block_specs, sample, sample, entire(pointwise_weight.shape),
                entire(x_table.shape), mine(scaled_table), others(scaled_table),
            ],
            out_specs=[entire(part_shape)] * 2 + [entire(field_shape)] * 2,
            scratch_shapes=u_scratch + t_scratch + spectrum_scratch + [pltpu.VMEM(field_shape, f32)],
        ),
        compiler_params=params,
        name="middle",
    )(place, *mixed, inputs, cotangent, pointwise_weight, x_table, scaled_table, scaled_table)
    again, own = lax.optimization_barrier((weight, own))
    slopes = to_owners(own, sent)
    local, *weights = pl.pallas_call(
        local_split_kernel,
        out_shape=[jax.ShapeDtypeStruct(field_shape, f32)] + [jax.ShapeDtypeStruct(weight_shape, bf16)] * 2,
        cost_estimate=estimate(6),
        compiler_params=mode_params,
        name="local",
    )(slope_high, slope_low, pointwise_weight, again)
    turned = mixing(adjoint_chunk, slopes, weights, "adjoint")

    block = 24 if modes % 24 == 0 else modes
    whole = jax.ShapeDtypeStruct(weight_shape, f32)
    weight_spec = pl.BlockSpec((block, channels, lanes), lambda i: (i, 0, 0))
    value_specs = [pl.BlockSpec(value.shape, lambda i: (0, 0, 0)) for value in owned]
    new_weight, new_first, new_second = pl.pallas_call(
        functools.partial(adam_kernel, len(owned)),
        out_shape=[whole] * 3,
        grid=(modes // block,),
        in_specs=value_specs * 2 + [weight_spec] * 3,
        out_specs=[weight_spec] * 3,
        scratch_shapes=[pltpu.VMEM((owners, rows, lanes), f32) for rows in (block, block, modes, modes)],
        compiler_params=pltpu.CompilerParams(vmem_limit_bytes=30 * 1024 * 1024),
        cost_estimate=pl.CostEstimate(flops=10**10, bytes_accessed=3 * 10**7, transcendentals=10**6),
        name="adam",
    )(*owned, *slopes, weight, first_moment.reshape(weight_shape), second_moment.reshape(weight_shape))
    mixed, new_first = from_owners(turned, last_order, new_first)

    out_field = pl.pallas_call(
        functools.partial(last_kernel, last_order),
        out_shape=jax.ShapeDtypeStruct(inputs.shape, bf16),
        grid_spec=pltpu.PrefetchScalarGridSpec(
            num_scalar_prefetch=1,
            grid=(1,),
            in_specs=[*block_specs, entire(field_shape), entire(x_inverse.shape), mine(plain_table), others(plain_table)],
            out_specs=sample,
            scratch_shapes=u_scratch + t_scratch + spectrum_scratch,
        ),
        compiler_params=params,
        name="last",
    )(place, *mixed, local, x_inverse, plain_table, plain_table)
    shape = spectral_weight.shape
    return (out_field, new_weight.reshape(shape), new_first.reshape(shape), new_second.reshape(shape))


def solution(mesh):
    return jax.shard_map(
        body,
        mesh=mesh,
        in_specs=(
            P(("grp", "dp"), "space", None, None),
            P(("grp", "dp"), "space", None, None),
            P(("grp", "space"), "dp", None, None, None),
            P(("grp", "space"), "dp", None, None, None),
            P(("grp", "space"), "dp", None, None, None),
            P("grp", None),
        ),
        out_specs=(
            P(("grp", "dp"), "space", None, None),
            P(("grp", "space"), "dp", None, None, None),
            P(("grp", "space"), "dp", None, None, None),
            P(("grp", "space"), "dp", None, None, None),
        ),
        check_vma=False,
    )
```

```python
import functools
import math

import jax
import jax.numpy as jnp
import ml_dtypes
import numpy as np
from jax import lax
from jax.experimental import pallas as pl
from jax.experimental.pallas import tpu as pltpu
from jax.sharding import PartitionSpec as P

MX = 16
MY = 16
MZ = 9
GX = 32
GY = 16
GZ = 32
HALF = MX // 2 + 1
CBLOCK = 16
ORDER = (0, 1, 2, 3, 4, 5, 6, 7)
BACK_ORDER = (6, 7, 5, 4, 3, 2, 1, 0)
LAST_ORDER = (1, 2, 6, 7, 5, 4, 3, 0)

beta_first = 0.9
beta_second = 0.999
learn_rate = 0.001
adam_epsilon = 1e-08
first_correct = 1.0 - math.exp(1000.0 * math.log(0.9))
second_correct = 1.0 - math.exp(1000.0 * math.log(0.999))

f32 = jnp.float32
bf16 = jnp.bfloat16


def split_np(table):
    high = table.astype(np.float32).astype(ml_dtypes.bfloat16)
    low = (table - high.astype(np.float64)).astype(np.float32).astype(ml_dtypes.bfloat16)
    return high, low


def parity_rows(per_group):
    half = per_group // 2 * MZ
    return [(slot % 2) * half + slot // 2 * MZ + kz for slot in range(per_group) for kz in range(MZ)]


def padded_rows(per_group):
    return -(-(per_group // 2 * MZ) // 8) * 8


def yz_tables(groups, scaled):
    per_group = MY // groups
    y_frequency = np.concatenate([np.arange(MY // 2), np.arange(GY - MY // 2, GY)]).reshape(groups, per_group // 2, 2)
    y_frequency = np.swapaxes(y_frequency, 1, 2)
    y_place = np.repeat(np.arange(GY // 2), GZ)
    z_place = np.tile(np.arange(GZ), GY // 2)
    turns = y_frequency[..., None, None] * y_place / GY + np.arange(MZ)[None, None, None, :, None] * z_place / GZ
    angle = 2.0 * np.pi * (turns % 1.0)
    table = np.stack([np.cos(angle), -np.sin(angle)], axis=2)
    if scaled:
        table = table * (np.where(np.arange(MZ) == 0, 1.0, 2.0) / (GX * GY * GZ))[:, None]
    table = table.reshape(groups, 2, 2, per_group // 2 * MZ, GY // 2 * GZ)
    rows = padded_rows(per_group)
    padded = np.zeros(table.shape[:3] + (rows, table.shape[-1]))
    padded[:, 0, :, : table.shape[3]] = table[:, 0]
    padded[:, 1, :, rows - table.shape[3] :] = table[:, 1]
    padded = padded.reshape(groups, 2, 2 * rows, table.shape[-1])
    return np.concatenate(split_np(padded), axis=2).reshape(groups, 8 * rows, table.shape[-1])


def x_tables(groups):
    width = GX // groups
    place = np.arange(width).reshape(1, 1, width)
    angle = 2.0 * np.pi * (np.arange(HALF)[None, :, None] * place % GX) / GX
    table = np.stack([np.cos(angle), -np.sin(angle)], axis=2).reshape(1, 2 * HALF, width)
    wide = np.einsum("gkx,cd->gkcxd", table, np.eye(CBLOCK)).reshape(1, 2 * HALF * CBLOCK, width * CBLOCK)
    high, low = split_np(wide)
    turned = np.swapaxes(np.concatenate([high, low, high], axis=1), 1, 2)
    return np.concatenate([high, low], axis=2)[0], np.ascontiguousarray(turned[0])


def dot(a, b):
    return lax.dot_general(a, b, (((1,), (0,)), ((), ())), preferred_element_type=f32)


def dot_nt(a, b):
    return lax.dot_general(a, b, (((1,), (1,)), ((), ())), preferred_element_type=f32)


def dot_tn(a, b):
    return lax.dot_general(a, b, (((0,), (0,)), ((), ())), preferred_element_type=f32)


def split(value):
    high = value.astype(bf16)
    return high, (value - high.astype(f32)).astype(bf16)


def lane_sign(shape, first):
    lane = lax.broadcasted_iota(jnp.int32, shape, len(shape) - 1)
    return jnp.where(lane < shape[-1] // 2, first, -first).astype(f32)


def swap(value):
    return pltpu.roll(value, value.shape[-1] // 2, value.ndim - 1)


def turning(space):
    return jnp.where(space == 1, -1.0, 1.0).astype(f32)


def to_spectra(turn, channels, fields, x_table, own, other, own_out, other_out, u_high, u_low, ready=None):
    for block in range(channels // CBLOCK):
        pieces = fields(block)
        cells = pieces[0].shape[0]
        result = dot(x_table[...], jnp.concatenate([pieces[0], pieces[0]], axis=0))
        if len(pieces) > 1:
            result = result + dot(x_table[:, :cells], pieces[1])
        middle = result.shape[-1] // 2
        lower, upper = result[:, :middle], result[:, middle:]
        high, low = split(jnp.concatenate([lower + upper, lower - upper], axis=1))
        rows = pl.ds(block * CBLOCK, CBLOCK)
        shape = (2 * HALF, CBLOCK, high.shape[-1])
        u_high[:, rows, :] = high.reshape(shape)
        u_low[:, rows, :] = low.reshape(shape)
    if ready is not None:
        ready()
    rows = own.shape[0] // 8
    part = 2 * rows
    count = own_out.shape[1]
    overlap = 2 * rows - count
    shared = pl.ds(count - rows, overlap)
    tables = [
        jnp.concatenate([own[2 * part * odd : 2 * part * (odd + 1), :], other[2 * part * odd : 2 * part * (odd + 1), :]], axis=0)
        for odd in range(2)
    ]
    briefs = [
        jnp.concatenate([own[2 * part * odd : 2 * part * odd + part, :], other[2 * part * odd : 2 * part * odd + part, :]], axis=0)
        for odd in range(2)
    ]
    width = 2 * channels
    sign = lane_sign((rows, width), -1.0)
    half_cells = u_high.shape[-1] // 2
    for first in range(0, HALF, 2):
        several = min(2, HALF - first)
        at = pl.ds(2 * first, 2 * several)
        high = u_high[at].reshape(several * width, 2 * half_cells)
        low = u_low[at].reshape(several * width, 2 * half_cells)
        wide = [dot_nt(tables[odd], high[:, half_cells * odd : half_cells * (odd + 1)]) for odd in range(2)]
        small = [dot_nt(briefs[odd], low[:, half_cells * odd : half_cells * (odd + 1)]) for odd in range(2)]
        for which, out in enumerate((own_out, other_out)):
            base = 2 * part * which
            totals = [
                (wide[odd][base : base + part] + wide[odd][base + part : base + 2 * part])
                + small[odd][part * which : part * (which + 1)]
                for odd in range(2)
            ]

            def put(kx, even, odd):
                out[kx, : count - rows] = even[: count - rows]
                out[kx, shared] = even[count - rows :] + odd[:overlap]
                out[kx, rows:] = odd[overlap:]

            for step in range(several):
                kx = first + step
                lanes = slice(step * width, (step + 1) * width)
                parts = [total[:, lanes] * turn if kx % 2 == 1 else total[:, lanes] for total in totals]
                real = [value[:rows] for value in parts]
                imag = [swap(value[rows:]) for value in parts]
                if kx < MX // 2:
                    put(kx, *[r + i * sign for r, i in zip(real, imag)])
                if kx > 0:
                    put(MX - kx, *[i - r * sign for r, i in zip(real, imag)])


def gather(place, order, sources, target):
    for step, source in zip(order, sources):
        block = source.shape[0]
        target[pl.ds((place[1] ^ step) * block, block)] = source[...]


def scatter(place, order, source, target):
    block = target.shape[1]
    for index, step in enumerate(order):
        target[index] = source[pl.ds((place[1] ^ step) * block, block)]


def from_spectra(turn, channels, own_in, other_in, back_to_cells, own, other, u_high, u_low, t_high, t_low):
    rows = own.shape[0] // 8
    part = 2 * rows
    count = own_in.shape[1]
    width = 2 * channels
    half_cells = own.shape[1]
    sign = lane_sign((count, width), -1.0)
    for kx in range(HALF):
        pieces = []
        for source in (own_in, other_in):
            if kx == 0:
                ahead = source[0]
                real, imag = ahead, ahead * sign
            elif kx == MX // 2:
                behind = source[MX - kx]
                real, imag = -behind * sign, behind
            else:
                ahead, behind = source[kx], source[MX - kx]
                real, imag = ahead - behind * sign, ahead * sign + behind
            if kx % 2 == 1:
                real, imag = real * turn, imag * turn
            pieces += [real, swap(imag)]
        at = pl.ds(kx * width, width)
        for odd, first in enumerate((0, count - rows)):
            turned = jnp.concatenate([piece[first : first + rows] for piece in pieces], axis=0).T
            high, low = split(turned)
            lanes = pl.ds(half_cells * odd, 2 * part)
            t_high[at, lanes] = high
            t_low[at, lanes] = low
    tables = []
    for odd in range(2):
        base = 2 * part * odd
        tables.append(
            [
                jnp.concatenate([own[base + shift : base + shift + part, :], other[base + shift : base + shift + part, :]], axis=0)
                for shift in (0, part)
            ]
        )
    several = 3 if HALF % 3 == 0 else 1
    for first in range(0, HALF, several):
        at = pl.ds(first * width, several * width)
        values = []
        for odd, (table_high, table_low) in enumerate(tables):
            lanes = pl.ds(half_cells * odd, 2 * part)
            high, low = t_high[at, lanes], t_low[at, lanes]
            values.append(dot(high, table_high) + dot(low, table_high) + dot(high, table_low))
        even, odd = values
        value_high, value_low = split(jnp.concatenate([even + odd, even - odd], axis=1))
        shape = (2 * several, channels, 2 * half_cells)
        u_high[pl.ds(2 * first, 2 * several)] = value_high.reshape(shape)
        u_low[pl.ds(2 * first, 2 * several)] = value_low.reshape(shape)


    def block(index):
        rows = pl.ds(index * CBLOCK, CBLOCK)
        shape = (2 * HALF * CBLOCK, u_high.shape[-1])
        high = u_high[:, rows, :].reshape(shape)
        low = u_low[:, rows, :].reshape(shape)
        return back_to_cells(high, low)

    return block


def first_kernel(
    order, field_in, x_in, table_in, own_part, other_part, field, x_table, own, other, sems, u_high, u_low, own_out, other_out
):
    blocks, width, _, cells = field.shape
    space = lax.axis_index("space")
    place = (space, lax.axis_index("dp") if len(order) > 1 else 0)
    copies = [pltpu.make_async_copy(x_in, x_table, sems.at[0])]
    for block in range(blocks):
        piece = field_in.at[0, :, pl.ds(block * CBLOCK, CBLOCK), :]
        copies.append(pltpu.make_async_copy(piece, field.at[block], sems.at[1 + block]))
    copies.append(pltpu.make_async_copy(table_in.at[space], own, sems.at[1 + blocks]))
    copies.append(pltpu.make_async_copy(table_in.at[1 - space], other, sems.at[2 + blocks]))
    for copy in copies:
        copy.start()
    copies[0].wait()

    def fields(block):
        copies[1 + block].wait()
        piece = field[block].reshape(width * CBLOCK, cells)
        return [piece]

    def ready():
        copies[1 + blocks].wait()
        copies[2 + blocks].wait()

    channels = blocks * CBLOCK
    to_spectra(turning(space), channels, fields, x_table, own, other, own_out, other_out, u_high, u_low, ready)
    scatter(place, order, other_out, other_part)
    scatter(place, order, own_out, own_part)


def middle_kernel(back_order, order, place, *refs):
    number = len(back_order)
    own_blocks, other_blocks = refs[:number], refs[number : 2 * number]
    field, cotangent, pointwise, x_table, own, other, *refs = refs[2 * number :]
    own_part, other_part, slope_high, slope_low, u_high, u_low, t_high, t_low, own_in, other_in, pre = refs
    gather(place, back_order, own_blocks, own_in)
    gather(place, back_order, other_blocks, other_in)
    width, channels, cells = field.shape
    places = x_table.shape[1] // 2
    turned = x_table[...].astype(f32).T.astype(bf16)

    def product(high, low):
        return (dot(turned[:places], high) + dot(turned[places:], high)) + dot(turned[:places], low)

    block = from_spectra(turning(place[0]), channels, own_in, other_in, product, own, other, u_high, u_low, t_high, t_low)
    for index in range(channels // CBLOCK):
        pre[:, pl.ds(index * CBLOCK, CBLOCK), :] = block(index).reshape(width, CBLOCK, cells)
    root = math.sqrt(2.0 / math.pi)
    mixer = jnp.concatenate(split(pointwise[...].T), axis=0)

    @pl.loop(0, width, unroll=4)
    def _(x):
        local = dot(mixer, field[x])
        value = pre[x] + (local[:channels] + local[channels:])
        square = value * value
        tanh = jnp.tanh(root * value * (1.0 + 0.044715 * square))
        slope = 0.5 * (1.0 + tanh) + (0.5 * root) * value * (1.0 - tanh * tanh) * (1.0 + 3.0 * 0.044715 * square)
        slope = slope * cotangent[x].astype(f32)
        high, low = split(slope)
        slope_high[x] = high
        slope_low[x] = low

    def fields(index):
        rows = pl.ds(index * CBLOCK, CBLOCK)
        shape = (width * CBLOCK, cells)
        high = slope_high[:, rows, :].reshape(shape)
        return [high, slope_low[:, rows, :].reshape(shape)]

    to_spectra(turning(place[0]), channels, fields, x_table, own, other, own_in, other_in, u_high, u_low)
    scatter(place, order, other_in, other_part)
    scatter(place, order, own_in, own_part)


def last_kernel(order, place, *refs):
    number = len(order)
    own_blocks, other_blocks = refs[:number], refs[number : 2 * number]
    local, x_inverse, own, other, out, u_high, u_low, t_high, t_low, own_in, other_in = refs[2 * number :]
    gather(place, order, own_blocks, own_in)
    gather(place, order, other_blocks, other_in)
    width, channels, cells = out.shape
    product = lambda high, low: dot(x_inverse[...], jnp.concatenate([high, high, low], axis=0))
    block = from_spectra(turning(place[0]), channels, own_in, other_in, product, own, other, u_high, u_low, t_high, t_low)
    for index in range(channels // CBLOCK):
        rows = pl.ds(index * CBLOCK, CBLOCK)
        value = block(index).reshape(width, CBLOCK, cells) + local[:, rows, :]
        out[:, rows, :] = value.astype(bf16)


def local_gradient(high_in, low_in, pointwise, out):
    channels = pointwise.shape[0]
    high, low = split(pointwise[...])
    both = jnp.concatenate([high, low], axis=0)

    @pl.loop(0, out.shape[0], unroll=4)
    def _(x):
        wide = dot(both, high_in[x])
        out[x] = (wide[:channels] + wide[channels:]) + dot(high, low_in[x])


def pairs_of(count):
    return [list(range(first, min(first + 2, count))) for first in range(0, count, 2)]


def spread_rows(rows, lower):
    if len(rows) == 1:
        half = rows[0].shape[-1] // 2
        return jnp.concatenate([rows[0][:, :half], rows[0][:, half:]], axis=0)
    zero = jnp.zeros_like(rows[0])
    one, two = rows
    return jnp.concatenate(
        [
            jnp.where(lower, one, zero),
            jnp.where(lower, swap(one), zero),
            jnp.where(lower, zero, swap(two)),
            jnp.where(lower, zero, two),
        ],
        axis=0,
    )


def lower_half(shape):
    return lax.broadcasted_iota(jnp.int32, shape, 1) < shape[1] // 2


def mode_chunk(modes):
    return 72 if modes % 72 == 0 else modes


def mode_rows(chunk):
    return parity_rows(chunk // MZ) if chunk > MZ else list(range(chunk))


def stack(refs, target):
    base = 0
    for ref in refs:
        target[pl.ds(base, ref.shape[0])] = ref[...]
        base += ref.shape[0]


def unstack(source, refs):
    base = 0
    for ref in refs:
        ref[...] = source[pl.ds(base, ref.shape[0])]
        base += ref.shape[0]


def split_kernel(weight, high, low):
    high[...], low[...] = split(weight[...])


def local_split_kernel(slope_high, slope_low, pointwise, weight, local, high, low):
    local_gradient(slope_high, slope_low, pointwise, local)
    modes = weight.shape[0]
    chunk = mode_chunk(modes)

    @pl.loop(0, modes // chunk)
    def _(index):
        at = pl.ds(index * chunk, chunk)
        high[at], low[at] = split(weight[at])


def mode_kernel(one_chunk, number, *refs):
    sources, weights, refs = refs[:number], refs[number : number + 2], refs[number + 2 :]
    spectra, out = refs[-2:]
    stack(sources, spectra)
    modes = spectra.shape[1]
    chunk = mode_chunk(modes)

    @pl.loop(0, modes // chunk)
    def _(index):
        start = index * chunk
        places = mode_rows(chunk)
        rows = [spectra[:, start + place, :] for place in places]

        def weight(first, count):
            values = [part[pl.ds(start + first, count)] for part in weights]
            return [value.reshape(-1, value.shape[-1]) for value in values]

        for place, value in zip(places, one_chunk(rows, weight)):
            out[:, start + place, :] = value

    unstack(out, refs[:number])


def mix_chunk(rows_of, weight):
    samples, width = rows_of[0].shape
    lower = lower_half((samples, width))
    sign = lane_sign((samples, width), -1.0)
    results = []
    for group in pairs_of(len(rows_of)):
        rows = spread_rows([rows_of[mode] for mode in group], lower)
        high, low = split(rows)
        block_high, block_low = weight(group[0], len(group))
        wide = dot(jnp.concatenate([high, low], axis=0), block_high)
        total = wide[: rows.shape[0]] + wide[rows.shape[0] :] + dot(high, block_low)
        for step, mode in enumerate(group):
            base = 2 * samples * step
            real, imag = total[base : base + samples], total[base + samples : base + 2 * samples]
            results.append(real + swap(imag) * sign)
    return results


def adjoint_chunk(rows_of, weight):
    samples, width = rows_of[0].shape
    lower = lower_half((samples, width))
    sign = lane_sign((samples, width), 1.0)
    results = []
    for group in pairs_of(len(rows_of)):
        rows = []
        for mode in group:
            rows += [rows_of[mode], swap(rows_of[mode]) * sign]
        rows = jnp.concatenate(rows, axis=0)
        high, low = split(rows)
        block_high, block_low = weight(group[0], len(group))
        wide = dot_nt(jnp.concatenate([high, low], axis=0), block_high)
        total = wide[: rows.shape[0]] + wide[rows.shape[0] :] + dot_nt(high, block_low)
        for step in range(len(group)):
            base = 2 * samples * step
            real, imag = total[base : base + samples], total[base + samples : base + 2 * samples]
            if len(group) == 1:
                results.append(jnp.concatenate([real, imag], axis=1))
            elif step == 0:
                results.append(jnp.where(lower, real, swap(imag)))
            else:
                results.append(jnp.where(lower, swap(real), imag))
    return results


def adam_kernel(number, *refs):
    spectra_parts, slope_parts, refs = refs[:number], refs[number : 2 * number], refs[2 * number :]
    weight, first, second, weight_out, first_out, second_out, spectra, slopes, all_spectra, all_slopes = refs
    samples, modes, width = spectra.shape
    start = pl.program_id(0) * modes

    @pl.when(pl.program_id(0) == 0)
    def _():
        places = mode_rows(mode_chunk(all_spectra.shape[1]))
        for parts, target in ((spectra_parts, all_spectra), (slope_parts, all_slopes)):
            base = 0
            for part in parts:
                for first in range(0, part.shape[1], MZ):
                    block = first // len(places) * len(places)
                    source = pl.ds(block + places[first - block], MZ)
                    target[pl.ds(base, part.shape[0]), pl.ds(first, MZ), :] = part[:, source, :]
                base += part.shape[0]

    here = pl.ds(pl.multiple_of(start, 8) if modes % 8 == 0 else 0, modes)
    spectra[...] = all_spectra[:, here, :]
    slopes[...] = all_slopes[:, here, :]
    lower = lower_half((samples, width))
    sign = lane_sign((samples, width), 1.0)
    for group in pairs_of(modes):
        left = spread_rows([spectra[:, mode, :] for mode in group], lower)
        right = []
        for mode in group:
            row = slopes[:, mode, :]
            right += [row, swap(row) * sign]
        right = jnp.concatenate(right, axis=0)
        left_high, left_low = split(left)
        right_high, right_low = split(right)
        gradient = dot_tn(
            jnp.concatenate([left_high, left_low, left_high], axis=0),
            jnp.concatenate([right_high, right_high, right_low], axis=0),
        )
        at = pl.ds(group[0], len(group))
        shape = (len(group),) + weight.shape[1:]
        gradient = gradient.reshape(shape)
        new_first = beta_first * first[at] + (1.0 - beta_first) * gradient
        new_second = beta_second * second[at] + (1.0 - beta_second) * gradient * gradient
        bottom = jnp.sqrt(new_second * (1.0 / second_correct)) + adam_epsilon
        first_out[at] = new_first
        second_out[at] = new_second
        weight_out[at] = weight[at] - (learn_rate / first_correct) * new_first / bottom


def body(inputs, cotangent, spectral_weight, first_moment, second_moment, pointwise_weight):
    groups = lax.axis_size("space")
    owners = lax.axis_size("dp")
    assert groups == 2 and inputs.shape[0] == 1
    per_group = MY // groups
    _, width, channels, cells = inputs.shape
    lanes = 2 * channels
    count = per_group * MZ
    pairs = spectral_weight.shape[1]
    modes = pairs * MZ
    paired = owners in (2, 4, 8)
    order, back_order, last_order = (
        [step for step in steps if step < owners] if paired else [0] for steps in (ORDER, BACK_ORDER, LAST_ORDER)
    )
    blocks = owners if paired else 1
    owner = lax.axis_index("dp").astype(jnp.int32)
    place = jnp.stack([lax.axis_index("space").astype(jnp.int32), owner if paired else jnp.int32(0)])

    plain_table = jnp.asarray(yz_tables(groups, False))
    scaled_table = jnp.asarray(yz_tables(groups, True))
    x_table, x_inverse = map(jnp.asarray, x_tables(groups))

    def mine(array):
        return pl.BlockSpec((None,) + array.shape[1:], lambda i, s: (s[0], 0, 0))

    def others(array):
        return pl.BlockSpec((None,) + array.shape[1:], lambda i, s: (1 - s[0], 0, 0))

    def entire(shape):
        return pl.BlockSpec(shape, lambda i, s: (0,) * len(shape))

    sample = pl.BlockSpec((None, width, channels, cells), lambda i, s: (0, 0, 0, 0))
    spectrum_shape = (MX, count, lanes)
    spectrum = jax.ShapeDtypeStruct(spectrum_shape, f32)
    field_shape = (width, channels, cells)
    u_scratch = [pltpu.VMEM((2 * HALF, channels, cells), bf16)] * 2
    t_scratch = [pltpu.VMEM((HALF * lanes, cells), bf16)] * 2
    params = pltpu.CompilerParams(vmem_limit_bytes=20 * 1024 * 1024)

    def other_core(value):
        return lax.ppermute(value, "space", [(0, 1), (1, 0)])

    spectrum_scratch = [pltpu.VMEM(spectrum_shape, f32)] * 2
    part_shape = (blocks, MX // blocks, count, lanes)
    block_specs = [entire(part_shape[1:])] * (2 * blocks)
    part_type = jax.ShapeDtypeStruct(part_shape, f32)
    table_scratch = pltpu.VMEM(plain_table.shape[1:], bf16)
    own, sent = pl.pallas_call(
        functools.partial(first_kernel, order),
        out_shape=[part_type] * 2,
        in_specs=[pl.BlockSpec(memory_space=pltpu.HBM)] * 3,
        scratch_shapes=[
            pltpu.VMEM((channels // CBLOCK, width, CBLOCK, cells), bf16),
            pltpu.VMEM(x_table.shape, bf16),
            table_scratch,
            table_scratch,
            pltpu.SemaphoreType.DMA((channels // CBLOCK + 3,)),
        ]
        + u_scratch
        + spectrum_scratch,
        compiler_params=pltpu.CompilerParams(vmem_limit_bytes=62 * 1024 * 1024),
        name="first",
    )(inputs, x_table, plain_table)

    weight_shape = (modes, channels, lanes)
    weight, own = lax.optimization_barrier((spectral_weight.reshape(weight_shape), own))

    def travel(value, step):
        return lax.ppermute(value, "dp", [(i, i ^ step) for i in range(owners)]) if step else value

    def to_owners(own, sent):
        got = other_core(sent)
        if not paired:
            total = own + got
            places = parity_rows(per_group)[::MZ]
            total = jnp.concatenate([total[:, :, place : place + MZ] for place in places], axis=2)
            return [lax.all_to_all(total.reshape(owners, modes, lanes), "dp", 0, 0, tiled=True)]
        return [travel((own[i] + got[i]).reshape(1, modes, lanes), step) for i, step in enumerate(order)]

    def from_owners(values, steps, tie=None):
        if not paired:
            value = lax.all_to_all(values[0], "dp", 0, 0, tiled=True).reshape(part_shape)
            slots = list(range(0, per_group, 2)) + list(range(1, per_group, 2))
            values = [jnp.concatenate([value[:, :, slot * MZ : (slot + 1) * MZ] for slot in slots], axis=2)]
        else:
            values = [travel(values[order.index(step)], step) for step in steps]
        if tie is not None:
            values, tie = lax.optimization_barrier((values, tie))
        values = [value.reshape(part_shape[1:]) for value in values]
        return values + [other_core(value) for value in values], tie

    mode_params = pltpu.CompilerParams(vmem_limit_bytes=14 * 1024 * 1024)

    def estimate(microseconds):
        return pl.CostEstimate(flops=microseconds * 10**9, bytes_accessed=10**5, transcendentals=0)

    def mixing(chunk, values, weights, name):
        return pl.pallas_call(
            functools.partial(mode_kernel, chunk, len(values)),
            out_shape=[jax.ShapeDtypeStruct(value.shape, f32) for value in values],
            scratch_shapes=[pltpu.VMEM((owners, modes, lanes), f32)] * 2,
            compiler_params=mode_params,
            cost_estimate=estimate(1),
            name=name,
        )(*values, *weights)

    large = 48 if modes % 48 == 0 else modes
    large_spec = pl.BlockSpec((large, channels, lanes), lambda i: (i, 0, 0))
    def split_weights(weight):
        return pl.pallas_call(
            split_kernel,
            out_shape=[jax.ShapeDtypeStruct(weight_shape, bf16)] * 2,
            grid=(modes // large,),
            in_specs=[large_spec],
            out_specs=[large_spec] * 2,
            compiler_params=mode_params,
            cost_estimate=estimate(6),
            name="split",
        )(weight)

    owned = to_owners(own, sent)
    mixture = list(mixing(mix_chunk, owned, split_weights(weight), "mix"))
    mixed, _ = from_owners(mixture, back_order)

    field = jax.ShapeDtypeStruct(field_shape, bf16)
    own, sent, slope_high, slope_low = pl.pallas_call(
        functools.partial(middle_kernel, back_order, order),
        out_shape=[part_type] * 2 + [field, field],
        grid_spec=pltpu.PrefetchScalarGridSpec(
            num_scalar_prefetch=1,
            grid=(1,),
            in_specs=[
                *block_specs, sample, sample, entire(pointwise_weight.shape),
                entire(x_table.shape), mine(scaled_table), others(scaled_table),
            ],
            out_specs=[entire(part_shape)] * 2 + [entire(field_shape)] * 2,
            scratch_shapes=u_scratch + t_scratch + spectrum_scratch + [pltpu.VMEM(field_shape, f32)],
        ),
        compiler_params=params,
        name="middle",
    )(place, *mixed, inputs, cotangent, pointwise_weight, x_table, scaled_table, scaled_table)
    again, own = lax.optimization_barrier((weight, own))
    slopes = to_owners(own, sent)
    local, *weights = pl.pallas_call(
        local_split_kernel,
        out_shape=[jax.ShapeDtypeStruct(field_shape, f32)] + [jax.ShapeDtypeStruct(weight_shape, bf16)] * 2,
        cost_estimate=estimate(6),
        compiler_params=mode_params,
        name="local",
    )(slope_high, slope_low, pointwise_weight, again)
    turned = mixing(adjoint_chunk, slopes, weights, "adjoint")

    block = 24 if modes % 24 == 0 else modes
    whole = jax.ShapeDtypeStruct(weight_shape, f32)
    weight_spec = pl.BlockSpec((block, channels, lanes), lambda i: (i, 0, 0))
    value_specs = [pl.BlockSpec(value.shape, lambda i: (0, 0, 0)) for value in owned]
    new_weight, new_first, new_second = pl.pallas_call(
        functools.partial(adam_kernel, len(owned)),
        out_shape=[whole] * 3,
        grid=(modes // block,),
        in_specs=value_specs * 2 + [weight_spec] * 3,
        out_specs=[weight_spec] * 3,
        scratch_shapes=[pltpu.VMEM((owners, rows, lanes), f32) for rows in (block, block, modes, modes)],
        compiler_params=pltpu.CompilerParams(vmem_limit_bytes=30 * 1024 * 1024),
        cost_estimate=pl.CostEstimate(flops=10**10, bytes_accessed=3 * 10**7, transcendentals=10**6),
        name="adam",
    )(*owned, *slopes, weight, first_moment.reshape(weight_shape), second_moment.reshape(weight_shape))
    mixed, new_first = from_owners(turned, last_order, new_first)

    out_field = pl.pallas_call(
        functools.partial(last_kernel, last_order),
        out_shape=jax.ShapeDtypeStruct(inputs.shape, bf16),
        grid_spec=pltpu.PrefetchScalarGridSpec(
            num_scalar_prefetch=1,
            grid=(1,),
            in_specs=[*block_specs, entire(field_shape), entire(x_inverse.shape), mine(plain_table), others(plain_table)],
            out_specs=sample,
            scratch_shapes=u_scratch + t_scratch + spectrum_scratch,
        ),
        compiler_params=params,
        name="last",
    )(place, *mixed, local, x_inverse, plain_table, plain_table)
    shape = spectral_weight.shape
    return (out_field, new_weight.reshape(shape), new_first.reshape(shape), new_second.reshape(shape))


def solution(mesh):
    return jax.shard_map(
        body,
        mesh=mesh,
        in_specs=(
            P(("grp", "dp"), "space", None, None),
            P(("grp", "dp"), "space", None, None),
            P(("grp", "space"), "dp", None, None, None),
            P(("grp", "space"), "dp", None, None, None),
            P(("grp", "space"), "dp", None, None, None),
            P("grp", None),
        ),
        out_specs=(
            P(("grp", "dp"), "space", None, None),
            P(("grp", "space"), "dp", None, None, None),
            P(("grp", "space"), "dp", None, None, None),
            P(("grp", "space"), "dp", None, None, None),
        ),
        check_vma=False,
    )
```
